256 devices in a mesh: gx: 16 (over y, x), gy: 16 (over z, core).
Axes of the slice: x: 4, y: 4, z: 8, core: 2. Of those that a mesh axis runs over, the one named last changes fastest.
Arguments:
- coarse_state: float32 [7, 96, 96, 384], P(None, 'gx', 'gy')
- fine_state: float32 [7, 524288], P(None, ('gx', 'gy'))
- patch_source: int32 [16, 16, 4], replicated, may hold values from 0 to 15, as said below
- patch_live: int32 [16, 16, 4], replicated, may hold values from 0 to 1, as said below
Outputs:
- coarse_out: float32 [7, 96, 96, 384], P(None, 'gx', 'gy')
- fine_out: float32 [7, 524288], P(None, ('gx', 'gy'))
The draws below stay inside these ranges and needn't reach their ends.
Inputs may be any that keep to these rules, and one draw needn't show every extreme that they name: For each gx index a and slot k, patch_source[a, :, k] names every gy index once; the live slots of one device name distinct tiles. A patch in slot k covers position k along the third dimension of its tile. `patch_live`: A device's live slots are its first ones; in every gx index at least one device has all 4 slots live, and every device has at least 1.
All inputs are finite; a program needn't handle non-finite values.
Results may differ from the reference program's by a relative error of at most 0.0003.
Values sent between devices are 32-bit elements; how exact they have to be, the bound alone decides.
A program may use at most 128 MiB of HBM per device.

```python
import jax
import jax.numpy as jnp
from jax import lax

FIELDS = 7
BOX = 4
CAP = 4
NX = 96
NY = 96
NZ = 384
FINE = 8
FINE_ROWS = 1024
N_GX = 16
N_GY = 16


def conserved(key, shape, power):
    keys = jax.random.split(key, 7)

    def unit(member):
        return jax.random.uniform(keys[member], shape, jnp.float32) ** power
    density = 1.0 + unit(0)
    velocity = [unit(1 + spatial) - 0.5 for spatial in range(3)]
    pressure = 0.5 + 1.5 * unit(4)
    energy = pressure / 0.4 + 0.5 * density * (velocity[0] * velocity[0] + velocity[1] * velocity[1] + velocity[2] * velocity[2])
    return jnp.stack([density, density * velocity[0], density * velocity[1], density * velocity[2], energy, density * 0.5 * unit(5), density * 0.5 * unit(6)])


def routing(key):
    row_keys = jax.random.split(key, N_GX)

    def one_row(row_key):
        pieces = jax.random.split(row_key, 5)
        outer_order = jax.random.permutation(pieces[0], N_GY).astype(jnp.int32)
        inner_order = jax.random.permutation(pieces[1], N_GY).astype(jnp.int32)
        shifts = jax.random.permutation(pieces[2], N_GY).astype(jnp.int32)[:CAP]
        owners = jnp.arange(N_GY, dtype=jnp.int32)
        source = outer_order[(inner_order[:, None] + shifts[None, :]) % N_GY]
        busiest = jax.random.randint(pieces[3], (), 0, N_GY, dtype=jnp.int32)
        loads = jnp.where(owners == busiest, CAP, jax.random.randint(pieces[4], (N_GY,), CAP - 3, CAP + 1, dtype=jnp.int32))
        live = (jnp.arange(CAP, dtype=jnp.int32)[None, :] < loads[:, None]).astype(jnp.int32)
        return (source.astype(jnp.int32), live)
    return jax.vmap(one_row)(row_keys)


def draw_coarse_state(key, part):
    key = jax.random.fold_in(key, 11)
    return conserved(key, (NX, NY, NZ), 1.0)


def draw_fine_state(key, part):
    key = jax.random.fold_in(key, 12)
    return conserved(key, (FINE_ROWS * FINE * FINE * FINE,), 1.0)


def draw_patch_source(key, part):
    shared = routing(key)
    return shared[0]


def draw_patch_live(key, part):
    shared = routing(key)
    return shared[1]


def setup_inputs(seed: int = 0) -> dict:
    key_list = jax.random.split(jax.random.key(seed), 5)
    return {
        "coarse_state": draw_coarse_state(jax.random.fold_in(key_list[4], 71), 0),
        "fine_state": draw_fine_state(jax.random.fold_in(key_list[4], 71), 0),
        "patch_source": draw_patch_source(jax.random.fold_in(key_list[4], 71), 0),
        "patch_live": draw_patch_live(jax.random.fold_in(key_list[4], 71), 0),
    }


GAMMA_MINUS = 0.4
WAVE_SPEED = 4.0
COURANT = 0.05
BURN_RATE = 10.0
HEAT_RELEASE = 2.0


def minmod(first_arg, second_arg):
    return 0.5 * (jnp.sign(first_arg) + jnp.sign(second_arg)) * jnp.minimum(jnp.abs(first_arg), jnp.abs(second_arg))


def euler_flux(fields, dim_index):
    density = fields[0]
    momentum = fields[1:4]
    velocity = fields[1 + dim_index] / density
    kinetic = 0.5 * (momentum[0] * momentum[0] + momentum[1] * momentum[1] + momentum[2] * momentum[2]) / density
    pressure = GAMMA_MINUS * (fields[4] - kinetic)
    rows_out = [fields[1 + dim_index]]
    for spatial in range(3):
        flux_term = momentum[spatial] * velocity
        if spatial == dim_index:
            flux_term = flux_term + pressure
        rows_out.append(flux_term)
    rows_out.append((fields[4] + pressure) * velocity)
    rows_out.append(fields[5] * velocity)
    rows_out.append(fields[6] * velocity)
    return jnp.stack(rows_out)


def face_fluxes(fields, direction):
    length = fields.shape[direction]
    jumps = lax.slice_in_dim(fields, 1, length, axis=direction) - lax.slice_in_dim(fields, 0, length - 1, axis=direction)
    slopes = minmod(lax.slice_in_dim(jumps, 0, length - 2, axis=direction), lax.slice_in_dim(jumps, 1, length - 1, axis=direction))
    left_state = lax.slice_in_dim(fields, 1, length - 2, axis=direction) + 0.5 * lax.slice_in_dim(slopes, 0, length - 3, axis=direction)
    right_state = lax.slice_in_dim(fields, 2, length - 1, axis=direction) - 0.5 * lax.slice_in_dim(slopes, 1, length - 2, axis=direction)
    return 0.5 * (euler_flux(left_state, direction - 1) + euler_flux(right_state, direction - 1)) - 0.5 * WAVE_SPEED * (right_state - left_state)


def reaction(fields):
    burned = BURN_RATE * fields[5]
    nothing = jnp.zeros_like(burned)
    return jnp.stack([nothing, nothing, nothing, nothing, HEAT_RELEASE * burned, -burned, burned])


def advance(padded, tstep):
    interior = padded[:, 2:-2, 2:-2, 2:-2]
    flux_x = face_fluxes(padded[:, :, 2:-2, 2:-2], 1)
    flux_y = face_fluxes(padded[:, 2:-2, :, 2:-2], 2)
    flux_z = face_fluxes(padded[:, 2:-2, 2:-2, :], 3)
    change = (flux_x[:, 1:] - flux_x[:, :-1]) + (flux_y[:, :, 1:] - flux_y[:, :, :-1]) + (flux_z[:, :, :, 1:] - flux_z[:, :, :, :-1])
    return interior - COURANT * change + tstep * reaction(interior), flux_x, flux_y, flux_z


def pair_sum(face_values):
    return face_values.reshape(FIELDS, BOX, 2, BOX, 2).sum(axis=(2, 4))


def patch_step(ghost, interior):
    padded = jnp.repeat(jnp.repeat(jnp.repeat(ghost, 2, axis=1), 2, axis=2), 2, axis=3)
    padded = padded.at[:, 2:-2, 2:-2, 2:-2].set(interior)
    updated, flux_x, flux_y, flux_z = advance(padded, 0.5 * COURANT)
    faces = jnp.stack([pair_sum(flux_x[:, 0]), pair_sum(flux_x[:, -1]), pair_sum(flux_y[:, :, 0]), pair_sum(flux_y[:, :, -1]), pair_sum(flux_z[:, :, :, 0]), pair_sum(flux_z[:, :, :, -1])], axis=1)
    return updated, faces


def settle_block(block, averaged, registers, coarse_faces, live):
    inside = slice(1, BOX + 1)
    far_end = BOX + 1
    whole = slice(None)
    interior = block[:, inside, inside, inside]
    block = block.at[:, inside, inside, inside].set(jnp.where(live, averaged, interior))
    positions = [(whole, 0, inside, inside), (whole, far_end, inside, inside), (whole, inside, 0, inside), (whole, inside, far_end, inside), (whole, inside, inside, 0), (whole, inside, inside, far_end)]
    for face_index in range(6):
        cell_value = block[positions[face_index]]
        fine_face = registers[:, face_index]
        if face_index % 2 == 0:
            moved = cell_value + COURANT * (coarse_faces[face_index] - fine_face)
        else:
            moved = cell_value + COURANT * (fine_face - coarse_faces[face_index])
        block = block.at[positions[face_index]].set(jnp.where(live, moved, cell_value))
    return block


def reference(coarse_state, fine_state, patch_source, patch_live):
    coarse_side = BOX + 2
    fine_side = 2 * BOX
    rimmed = jnp.pad(coarse_state, ((0, 0), (2, 2), (2, 2), (2, 2)), mode="wrap")
    advanced, flux_x, flux_y, flux_z = advance(rimmed, COURANT)
    fine_all = fine_state.reshape(FIELDS, FINE_ROWS, fine_side, fine_side, fine_side)
    zero = jnp.int32(0)

    def locate(row):
        row = row.astype(jnp.int32)
        row_gx = row // (N_GY * CAP)
        owner_gy = (row // CAP) % N_GY
        slot_index = row % CAP
        source = patch_source[row_gx, owner_gy, slot_index].astype(jnp.int32)
        live = patch_live[row_gx, owner_gy, slot_index] == 1
        return row, row_gx * coarse_side, source * coarse_side, slot_index * coarse_side, live

    def one_patch(row):
        row, base_x, base_y, base_z, live = locate(row)
        extent = (FIELDS, coarse_side, coarse_side, coarse_side)
        old_box = jnp.where(live, lax.dynamic_slice(coarse_state, (zero, base_x, base_y, base_z), extent), 1.0)
        new_box = jnp.where(live, lax.dynamic_slice(advanced, (zero, base_x, base_y, base_z), extent), 1.0)
        interior = lax.dynamic_index_in_dim(fine_all, row, axis=1, keepdims=False)
        first, faces_one = patch_step(old_box, interior)
        second, faces_two = patch_step(0.5 * (old_box + new_box), first)
        averaged = second.reshape(FIELDS, BOX, 2, BOX, 2, BOX, 2).mean(axis=(2, 4, 6))
        registers = 0.125 * (faces_one + faces_two)
        return jnp.where(live, second, interior), averaged, registers

    rows = jnp.arange(FINE_ROWS, dtype=jnp.int32).reshape(FINE_ROWS // CAP, CAP)
    fine_new, averages, regs = lax.map(jax.vmap(one_patch), rows)
    fine_new = fine_new.reshape((FINE_ROWS,) + fine_new.shape[2:])
    averages = averages.reshape((FINE_ROWS,) + averages.shape[2:])
    regs = regs.reshape((FINE_ROWS,) + regs.shape[2:])
    fine_out = jnp.transpose(fine_new, (1, 0, 2, 3, 4)).reshape(FIELDS, FINE_ROWS * fine_side * fine_side * fine_side)

    def settle_row(row, grid):
        row, base_x, base_y, base_z, live = locate(row)
        extent = (FIELDS, coarse_side, coarse_side, coarse_side)
        block = lax.dynamic_slice(grid, (zero, base_x, base_y, base_z), extent)
        x_low = lax.dynamic_slice(flux_x, (zero, base_x + 1, base_y + 1, base_z + 1), (FIELDS, 1, BOX, BOX))[:, 0]
        x_high = lax.dynamic_slice(flux_x, (zero, base_x + BOX + 1, base_y + 1, base_z + 1), (FIELDS, 1, BOX, BOX))[:, 0]
        y_low = lax.dynamic_slice(flux_y, (zero, base_x + 1, base_y + 1, base_z + 1), (FIELDS, BOX, 1, BOX))[:, :, 0]
        y_high = lax.dynamic_slice(flux_y, (zero, base_x + 1, base_y + BOX + 1, base_z + 1), (FIELDS, BOX, 1, BOX))[:, :, 0]
        z_low = lax.dynamic_slice(flux_z, (zero, base_x + 1, base_y + 1, base_z + 1), (FIELDS, BOX, BOX, 1))[:, :, :, 0]
        z_high = lax.dynamic_slice(flux_z, (zero, base_x + 1, base_y + 1, base_z + BOX + 1), (FIELDS, BOX, BOX, 1))[:, :, :, 0]
        averaged = lax.dynamic_index_in_dim(averages, row, axis=0, keepdims=False)
        registers = lax.dynamic_index_in_dim(regs, row, axis=0, keepdims=False)
        block = settle_block(block, averaged, registers, [x_low, x_high, y_low, y_high, z_low, z_high], live)
        return lax.dynamic_update_slice(grid, block, (zero, base_x, base_y, base_z))

    coarse_out = lax.fori_loop(0, FINE_ROWS, settle_row, advanced)
    return coarse_out, fine_out
```

```python
import jax
import jax.numpy as jnp
from jax import lax
from jax.experimental import pallas as pl
from jax.experimental.pallas import tpu as pltpu
from jax.sharding import PartitionSpec as P

F = 7
CAP = 4
SIDE = 6
L = 128
F32 = jnp.float32
BF16 = jnp.bfloat16
MESH = pl.DeviceIdType.MESH


def iota(shape, dim):
    return lax.broadcasted_iota(jnp.int32, shape, dim)


def take(ref, start, count, stride):
    return ref.reshape(ref.size // L, L)[pl.ds(start, count, stride=stride), :]


def put(ref, start, count, stride, value):
    ref.reshape(ref.size // L, L)[pl.ds(start, count, stride=stride), :] = value


def exact_dot(a, e):
    hi = a.astype(BF16)
    rest = a - hi.astype(F32)
    mid = rest.astype(BF16)
    low = (rest - mid.astype(F32)).astype(BF16)
    out = jnp.dot(hi, e, preferred_element_type=F32)
    out = out + jnp.dot(mid, e, preferred_element_type=F32)
    return out + jnp.dot(low, e, preferred_element_type=F32)


def minmod(a, b):
    return jnp.maximum(jnp.minimum(a, b), 0.0) + jnp.minimum(jnp.maximum(a, b), 0.0)


def half_flux(u, d):
    inv = 1.0 / u[0]
    kk = u[1] * u[1] + u[2] * u[2] + u[3] * u[3]
    p = 0.4 * u[4] - 0.2 * (kk * inv)
    scaled = 0.025 * u[1 + d]
    v = scaled * inv
    out = [scaled]
    for i in range(3):
        term = u[1 + i] * v
        if i == d:
            term = term + 0.025 * p
        out.append(term)
    out += [(u[4] + p) * v, u[5] * v, u[6] * v]
    return out


def split_flux(um, u, up, d):
    h = [0.5 * minmod(c - m, q - c) for m, c, q in zip(um, u, up)]
    left = [c + s for c, s in zip(u, h)]
    right = [c - s for c, s in zip(u, h)]
    plus = [f + 0.1 * c for f, c in zip(half_flux(left, d), left)]
    minus = [f - 0.1 * c for f, c in zip(half_flux(right, d), right)]
    return plus, minus


def react(u, change, t):
    burned = (10.0 * t) * u[5]
    new = [c - g for c, g in zip(u, change)]
    new[4] = new[4] + 2.0 * burned
    new[5] = new[5] - burned
    new[6] = new[6] + burned
    return new


def make_kernel(n_gx, n_gy):
    def kernel(
        coarse, fine, source, live, coarse_out, fine_out,
        S, FIN, BASE, NEWC, WN, PZ, MZ, CM, BB, MO, MN, GL, FS, FT, GG, SB1, RB1, SB2, RB2,
        EZ, EG, WD, WX, E2, E2X, LW, TT, src_s, live_s, kf_s, kg_s,
        in_sem, fin_sem, tab_sem, h_send, h_recv, m_send, m_recv,
    ):
        a = lax.axis_index("gx")
        b = lax.axis_index("gy")
        up_a, dn_a = lax.rem(a + 1, n_gx), lax.rem(a + n_gx - 1, n_gx)
        up_b, dn_b = lax.rem(b + 1, n_gy), lax.rem(b + n_gy - 1, n_gy)

        tabs = [
            pltpu.make_async_copy(source.at[a], src_s, tab_sem.at[0]),
            pltpu.make_async_copy(live.at[a], live_s, tab_sem.at[1]),
        ]
        for cp in tabs:
            cp.start()
        own = []
        for j in range(3):
            cp = pltpu.make_async_copy(
                coarse.at[:, :, :, pl.ds(j * L, L)],
                S.at[2:8, 2:8, j, 0:F, :],
                in_sem.at[j],
            )
            cp.start()
            own.append(cp)
        fin_cp = pltpu.make_async_copy(fine, FIN, fin_sem)
        fin_cp.start()

        barrier = pltpu.get_barrier_semaphore()
        for d in (up_a, dn_a):
            pl.semaphore_signal(barrier, inc=1, device_id=(d, b), device_id_type=MESH)

        def greet(o, _):
            pl.semaphore_signal(
                barrier, inc=1, device_id=(a, lax.rem(b + o, n_gy)), device_id_type=MESH
            )
            return 0

        lax.fori_loop(1, n_gy, greet, 0)

        row = iota((L, L), 0)
        col = iota((L, L), 1)
        c32 = col & 31
        s32 = col >> 5
        zc = jnp.where(
            c32 < 4, 0, jnp.where(c32 < 8, 5, jnp.where(c32 < 12, c32 - 7, jnp.where(c32 < 16, c32 - 11, (c32 & 3) + 1)))
        )
        EZ[...] = (row == 6 * s32 + zc).astype(F32).astype(BF16)
        fy = (col >> 3) & 7
        fz = col & 7
        cz, cy = fz >> 1, fy >> 1
        EG[:, 0:L] = (row == jnp.where(fz < 4, 0, 4) + cy).astype(F32).astype(BF16)
        EG[:, L : 2 * L] = (row == jnp.where(fy < 4, 8, 12) + cz).astype(F32).astype(BF16)
        EG[:, 2 * L : 3 * L] = (row == 16 + cy * 4 + cz).astype(F32).astype(BF16)
        ry = (row >> 3) & 7
        rz = row & 7
        rzc, ryc = rz >> 1, ry >> 1
        e6 = (c32 * 43) >> 8
        eyv = jnp.where(c32 < 24, e6 + 1, jnp.where(c32 < 28, 0, 5))
        ezv = jnp.where(c32 < 24, c32 - 6 * e6, (c32 & 3) + 1)
        main = c32 < 24
        wa = main & (ezv >= 1) & (ezv <= 4) & (ryc == eyv - 1) & (rzc == ezv - 1)
        wz = main & (ryc == eyv - 1) & (((ezv == 0) & (rz == 0)) | ((ezv == 5) & (rz == 7)))
        wy = (
            jnp.logical_not(main)
            & (rzc == ezv - 1)
            & (((eyv == 0) & (ry == 0)) | ((eyv == 5) & (ry == 7)))
        )
        for i, w in enumerate((wa, wz, wy)):
            WD[i * L : (i + 1) * L, :] = jnp.where(w, 0.125, 0.0).astype(BF16)
        WX[...] = jnp.where((ryc == (c32 >> 2)) & (rzc == (c32 & 3)), 0.125, 0.0).astype(BF16)
        r32 = row & 31
        rs = row >> 5
        r6 = (r32 * 43) >> 8
        rzv = jnp.where(r32 < 24, r32 - 6 * r6, (r32 & 3) + 1)
        E2[...] = (col == 6 * rs + rzv).astype(F32).astype(BF16)
        E2X[...] = (col == 6 * rs + (r32 & 3) + 1).astype(F32).astype(BF16)

        for cp in tabs:
            cp.wait()

        def route(o, carry):
            owner, alive = carry
            d = lax.rem(b + o, n_gy)
            kf = jnp.int32(0)
            kg = jnp.int32(0)
            back = lax.rem(n_gy - o, n_gy)
            own_new, live_new = [], []
            for k in reversed(range(CAP)):
                kf = jnp.where((src_s[k, b] == d) & (live_s[k, b] == 1), k, kf)
                mine = src_s[k, d] == b
                lv = live_s[k, d]
                kg = jnp.where(mine & (lv == 1), k, kg)
                own_new.append(jnp.where(mine, back, owner[k]))
                live_new.append(jnp.where(mine, lv, alive[k]))
            kf_s[o] = kf
            kg_s[o] = kg
            return tuple(reversed(own_new)), tuple(reversed(live_new))

        zeros = (jnp.int32(0),) * CAP
        owner, alive = lax.fori_loop(0, n_gy, route, (zeros, zeros))

        for cp in own:
            cp.wait()
        pl.semaphore_wait(barrier, n_gy + 1)

        halos = []
        for j in range(3):
            for h, (src_x, dst_x, src_y, dst_y, dev) in enumerate(
                (
                    ((6, 8), (0, 2), (2, 8), (2, 8), (up_a, b)),
                    ((2, 4), (8, 10), (2, 8), (2, 8), (dn_a, b)),
                    ((2, 8), (2, 8), (6, 8), (0, 2), (a, up_b)),
                    ((2, 8), (2, 8), (2, 4), (8, 10), (a, dn_b)),
                )
            ):
                cp = pltpu.make_async_remote_copy(
                    src_ref=S.at[src_x[0] : src_x[1], src_y[0] : src_y[1], j, 0:F, :],
                    dst_ref=S.at[dst_x[0] : dst_x[1], dst_y[0] : dst_y[1], j, 0:F, :],
                    send_sem=h_send.at[j, h],
                    recv_sem=h_recv.at[j, h],
                    device_id=dev,
                    device_id_type=MESH,
                )
                cp.start()
                halos.append(cp)

        lane = iota((8, L), 1)
        sub = iota((8, L), 0)
        lc = lane & 31
        ls = lane >> 5
        ly = jnp.where(
            lc < 4, lc + 1, jnp.where(lc < 8, lc - 3, jnp.where(lc < 12, 0, jnp.where(lc < 16, 5, ((lc - 16) >> 2) + 1)))
        )
        low16 = lc < 16

        def ghost_messages(tiles, dst):
            BB[...] = exact_dot(tiles.reshape(SIDE * SIDE * 8, L), EZ[...]).reshape(SIDE, SIDE, 8, L)
            merged = []
            for X in range(4):
                acc = BB[X + 1, 0]
                for y in range(1, 6):
                    acc = jnp.where(low16 & (ly == y), BB[X + 1, y], acc)
                if X in (0, 3):
                    for y in range(1, 5):
                        acc = jnp.where(
                            jnp.logical_not(low16) & (ly == y), BB[0 if X == 0 else 5, y], acc
                        )
                merged.append(acc)
            for k in range(CAP):
                acc = None
                for X in range(4):
                    shift = (32 * (X - k)) % L
                    part = merged[X] if shift == 0 else pltpu.roll(merged[X], shift, 1)
                    acc = part if acc is None else jnp.where(ls == X, part, acc)
                dst[k] = acc

        ghost_messages(S[2:8, 2:8, 0], MO)
        fin_cp.wait()
        for t in range(4 * CAP):
            FT[t // 4, t % 4, 0:F, :] = FIN[:, t * L : (t + 1) * L]

        def fill1(o, buf):
            buf[o, 0:4] = FT[kf_s[o]]
            buf[o, 4] = MO[kg_s[o]]

        fill1(0, RB1)

        def send1(o, _):
            fill1(o, SB1)
            pltpu.make_async_remote_copy(
                src_ref=SB1.at[o],
                dst_ref=RB1.at[o],
                send_sem=m_send.at[0],
                recv_sem=m_recv.at[0],
                device_id=(a, lax.rem(b + o, n_gy)),
                device_id_type=MESH,
            ).start()
            return 0

        lax.fori_loop(1, n_gy, send1, 0)


        def cells(x, y, j):
            start = (((x + 2) * 10 + (y + 2)) * 3 + j) * 8
            return [take(S, start + f, 8, 24) for f in range(F)]

        for x in range(SIDE):
            for y in range(SIDE):
                WN[x, y] = jnp.where(lane < L - 2, S[x + 2, y + 2, 0], S[x + 2, y + 2, 2])
        for cp in halos[:4]:
            cp.wait_recv()

        slot24 = (lane >= 6).astype(jnp.int32) + (lane >= 12).astype(jnp.int32) + (lane >= 18).astype(jnp.int32)
        zpos = lane - 6 * slot24
        alive_lane = jnp.where(
            slot24 == 0, alive[0], jnp.where(slot24 == 1, alive[1], jnp.where(slot24 == 2, alive[2], alive[3]))
        )
        live_z = (lane < 24) & (alive_lane == 1)
        zin = live_z & (zpos >= 1) & (zpos <= 4)
        yin = (sub >= 1) & (sub <= 4)
        inner = yin & zin
        y_low, y_high = (sub == 0) & zin, (sub == 5) & zin
        z_low, z_high = yin & live_z & (zpos == 0), yin & live_z & (zpos == 5)

        def y_parts(x, j):
            plus, minus = split_flux(cells(x, -2, j), cells(x, -1, j), cells(x, 0, j), 1)
            g = [p + pltpu.roll(m, 7, 0) for p, m in zip(plus, minus)]
            return g, [pltpu.roll(v, 7, 0) for v in g]

        def z_circle(left_edge, mid, right_edge):
            um = [pltpu.roll(jnp.where(lane == L - 1, l, c), 1, 1) for l, c in zip(left_edge, mid)]
            up = [pltpu.roll(jnp.where(lane == 0, r, c), L - 1, 1) for r, c in zip(right_edge, mid)]
            return split_flux(um, mid, up, 2)

        def x_fluxes(j):
            faces = []
            before = None
            um, u = cells(-2, 0, j), cells(-1, 0, j)
            for x in range(-1, 7):
                up = cells(x + 1, 0, j)
                plus, minus = split_flux(um, u, up, 0)
                if before is not None:
                    faces.append([p + m for p, m in zip(before, minus)])
                before = plus
                um, u = u, up
                if len(faces) >= 2:
                    yield x - 1, faces[-2], faces[-1]

        for x, lower, upper in x_fluxes(0):
            u = cells(x, 0, 0)
            y_lo, y_up = y_parts(x, 0)
            circle = [take(WN, x * 64 + f, 8, 8) for f in range(F)]
            plus, minus = z_circle(circle, circle, circle)
            change, masked = [], []
            for f in range(F):
                g = plus[f] + pltpu.roll(minus[f], L - 1, 1)
                dz = g - pltpu.roll(g, 1, 1)
                dx = upper[f] - lower[f]
                dy = y_up[f] - y_lo[f]
                change.append(dx + dy + dz)
                if x == 0:
                    dxm = jnp.where(inner, 0.0, upper[f]) - lower[f]
                    dym = dy
                elif x == 5:
                    dxm = upper[f] - jnp.where(inner, 0.0, lower[f])
                    dym = dy
                else:
                    dxm = dx
                    dym = jnp.where(y_low, 0.0, y_up[f]) - jnp.where(y_high, 0.0, y_lo[f])
                masked.append(dxm + dym)
            new = react(u, change, 0.05)
            for f in range(F):
                put(NEWC, x * 64 + f, 8, 8, new[f])
                CM[x, f] = masked[f]

        ghost_messages(NEWC[:, 0:SIDE], MN)
        RB2[0] = MN[kg_s[0]]

        def send2(o, _):
            SB2[o] = MN[kg_s[o]]
            pltpu.make_async_remote_copy(
                src_ref=SB2.at[o],
                dst_ref=RB2.at[o],
                send_sem=m_send.at[1],
                recv_sem=m_recv.at[1],
                device_id=(a, lax.rem(b + o, n_gy)),
                device_id_type=MESH,
            ).start()
            return 0

        lax.fori_loop(1, n_gy, send2, 0)

        for cp in halos[4:]:
            cp.wait_recv()

        def z_parts(j, _):
            jm, jp = lax.rem(j + 2, 3), lax.rem(j + 1, 3)
            for x in range(SIDE):
                plus, minus = z_circle(cells(x, 0, jm), cells(x, 0, j), cells(x, 0, jp))
                for f in range(F):
                    PZ[j, x, f] = plus[f]
                    MZ[j, x, f] = minus[f]
            return 0

        lax.fori_loop(0, 3, z_parts, 0)

        def z_faces(x, f, j):
            jm, jp = lax.rem(j + 2, 3), lax.rem(j + 1, 3)
            p, m = PZ[j, x, f], MZ[j, x, f]
            upper = p + pltpu.roll(jnp.where(lane == 0, MZ[jp, x, f], m), L - 1, 1)
            lower = m + pltpu.roll(jnp.where(lane == L - 1, PZ[jm, x, f], p), 1, 1)
            return lower, upper

        def store(x, j, new):
            for f in range(F):
                put(BASE, (x * 24 + j) * 8 + f, 8, 24, new[f])

        zero = jnp.int32(0)
        for x in range(SIDE):
            change = []
            for f in range(F):
                lower, upper = z_faces(x, f, zero)
                if 1 <= x <= 4:
                    lower = jnp.where(z_high, 0.0, lower)
                    upper = jnp.where(z_low, 0.0, upper)
                change.append(CM[x, f] + (upper - lower))
            store(x, zero, react(cells(x, 0, 0), change, 0.05))

        def rest(j, _):
            for x, lower, upper in x_fluxes(j):
                y_lo, y_up = y_parts(x, j)
                change = []
                for f in range(F):
                    z_lo, z_up = z_faces(x, f, j)
                    change.append((upper[f] - lower[f]) + (y_up[f] - y_lo[f]) + (z_up - z_lo))
                store(x, j, react(cells(x, 0, j), change, 0.05))
            return 0

        lax.fori_loop(1, 3, rest, 0)

        def wait_messages(buf, i):
            whole = buf.at[1:n_gy]
            pltpu.make_async_copy(whole, whole, m_recv.at[i]).wait()

        my_src = [lax.rem(b + n_gy - src_s[k, b], n_gy) for k in range(CAP)]
        my_live = [live_s[k, b] for k in range(CAP)]

        def ghost_fields(messages):
            for k in range(2 * CAP):
                for X in range(4):
                    tile = messages[k]
                    GL[k, X] = tile if X == 0 else pltpu.roll(tile, L - 32 * X, 1)
            expanded = exact_dot(GL[...].reshape(2 * CAP * 32, L), EG[...])
            for i in range(3):
                GG[i] = expanded[:, i * L : (i + 1) * L]
            return [[GG[i, pl.ds(f, 8 * CAP, stride=8), :] for f in range(F)] for i in range(3)]

        wait_messages(RB1, 0)
        for k in range(CAP):
            FS[k] = RB1[owner[k], 0:4]
            FS[CAP + k] = FT[k]
        R = 8 * CAP
        flane = iota((R, L), 1)
        frow = iota((R, L), 0) & 3
        fz1, fy1, fxb = flane & 7, (flane >> 3) & 7, flane >> 6
        at_z0, at_z7 = fz1 == 0, fz1 == 7
        at_y0, at_y7 = fy1 == 0, fy1 == 7
        odd = fxb == 1
        first_row, last_row = frow == 0, frow == 3
        at_x0 = first_row & jnp.logical_not(odd)
        at_x7 = last_row & odd

        def lane_down(step):
            return lambda v: pltpu.roll(v, step, 1)

        def lane_up(step):
            return lambda v: pltpu.roll(v, L - step, 1)

        def x_down(v):
            r = pltpu.roll(v, 64, 1)
            return jnp.where(odd, r, pltpu.roll(r, 1, 0))

        def x_up(v):
            r = pltpu.roll(v, 64, 1)
            return jnp.where(odd, pltpu.roll(r, R - 1, 0), r)

        plan = (
            (2, 0, lane_down(1), lane_up(1), at_z0, at_z7, fz1 < 4),
            (1, 1, lane_down(8), lane_up(8), at_y0, at_y7, fy1 < 4),
            (0, 2, x_down, x_up, at_x0, at_x7, jnp.logical_not(odd)),
        )

        def substep(u, ghosts):
            change = None
            faces = []
            for d, gi, down, upw, at_lo, at_hi, lo_side in plan:
                g = ghosts[gi]
                um = [jnp.where(at_lo, w, down(c)) for c, w in zip(u, g)]
                up = [jnp.where(at_hi, w, upw(c)) for c, w in zip(u, g)]
                plus, minus = split_flux(um, u, up, d)
                sign = jnp.where(lo_side, 0.1, -0.1)
                edge = [h + sign * c for h, c in zip(half_flux(g, d), g)]
                lower, upper = [], []
                for f in range(F):
                    lower.append(minus[f] + jnp.where(at_lo, edge[f], down(plus[f])))
                    upper.append(plus[f] + jnp.where(at_hi, edge[f], upw(minus[f])))
                diff = [q - p for q, p in zip(upper, lower)]
                change = diff if change is None else [c + v for c, v in zip(change, diff)]
                faces.append(
                    [
                        jnp.where(at_lo[0:16], -p[0:16], jnp.where(at_hi[0:16], q[0:16], 0.0))
                        for q, p in zip(upper, lower)
                    ]
                )
            return react(u, change, 0.025), faces

        old = [MO[k] for k in range(CAP)] + [RB1[my_src[k], 4] for k in range(CAP)]
        u0 = [take(FS, f, R, 8) for f in range(F)]
        u1, faces1 = substep(u0, ghost_fields(old))
        for f in range(F):
            put(FS, f, R, 8, u1[f])
            for i in range(3):
                LW[1 + i, pl.ds(f, 16, stride=8), :] = faces1[i][f]

        wait_messages(RB2, 1)
        new = [MN[k] for k in range(CAP)] + [RB2[my_src[k]] for k in range(CAP)]
        old = [MO[k] for k in range(CAP)] + [RB1[my_src[k], 4] for k in range(CAP)]
        mean = [0.5 * (o + n) for o, n in zip(old, new)]
        u1 = [take(FS, f, R, 8) for f in range(F)]
        u2, faces2 = substep(u1, ghost_fields(mean))
        for f in range(F):
            put(FS, f, R, 8, u2[f])
            LW[0, pl.ds(f, 16, stride=8), :] = u2[f][0:16]
            for i in range(3):
                rows = pl.ds(f, 16, stride=8)
                LW[1 + i, rows, :] = LW[1 + i, rows, :] + faces2[i][f]

        for t in range(4 * CAP):
            k = t // 4
            fine_out[:, t * L : (t + 1) * L] = jnp.where(
                my_live[k] == 1, FS[CAP + k, t % 4, 0:F, :], FT[k, t % 4, 0:F, :]
            )

        TT[0] = exact_dot(jnp.concatenate([LW[0], LW[1], LW[2]], axis=1), WD[...])
        TT[1] = exact_dot(LW[3], WX[...])
        slot_live = jnp.where(ls == 0, alive[0], jnp.where(ls == 1, alive[1], jnp.where(ls == 2, alive[2], alive[3])))
        keep = slot_live == 1

        def by_slot(i, X):
            acc = TT[i, pl.ds(X * 8, 8), :]
            for k in range(1, CAP):
                acc = jnp.where(ls == k, TT[i, pl.ds((k * 4 + X) * 8, 8), :], acc)
            return jnp.where(keep, acc, 0.0)

        l6 = (lc * 43) >> 8
        lyv = jnp.where(lc < 24, l6 + 1, jnp.where(lc < 28, 0, 5))
        blocks = []
        for X in range(4):
            t = by_slot(0, X)
            for y in range(6):
                blocks.append(jnp.where(lyv == y, t, 0.0))
        inside = exact_dot(jnp.concatenate(blocks, axis=0), E2[...])
        lxy = (lc >> 2) + 1
        blocks = []
        for X in (0, 3):
            t = by_slot(1, X)
            for y in range(1, 5):
                blocks.append(jnp.where(lxy == y, t, 0.0))
        across = exact_dot(jnp.concatenate(blocks, axis=0), E2X[...])
        for x in range(SIDE):
            for y in range(SIDE):
                tile = BASE[x, y, 0]
                if 1 <= x <= 4:
                    i = ((x - 1) * 6 + y) * 8
                    part = inside[i : i + 8]
                    if 1 <= y <= 4:
                        tile = jnp.where(zin, part, tile + part)
                    else:
                        tile = tile + part
                elif 1 <= y <= 4:
                    i = ((0 if x == 0 else 4) + y - 1) * 8
                    tile = tile + across[i : i + 8]
                coarse_out[x, y, :, 0:L] = tile[0:F]
                for j in (1, 2):
                    coarse_out[x, y, :, j * L : (j + 1) * L] = BASE[x, y, j, 0:F]

        for cp in halos:
            cp.wait_send()
        for i, buf in enumerate((SB1, SB2)):
            whole = buf.at[1:n_gy]
            pltpu.make_async_copy(whole, whole, m_send.at[i]).wait()

    return kernel


def solution(mesh):
    n_gx, n_gy = mesh.shape["gx"], mesh.shape["gy"]
    kernel = make_kernel(n_gx, n_gy)

    def local(coarse_state, fine_state, patch_source, patch_live):
        coarse = jnp.transpose(coarse_state, (1, 2, 0, 3))
        source = jnp.transpose(patch_source, (0, 2, 1))
        live = jnp.transpose(patch_live, (0, 2, 1))
        v = pltpu.VMEM
        anywhere = pl.BlockSpec(memory_space=pl.ANY)
        vmem = pl.BlockSpec(memory_space=pltpu.VMEM)
        coarse_out, fine_out = pl.pallas_call(
            kernel,
            out_shape=(
                jax.ShapeDtypeStruct(coarse.shape, F32),
                jax.ShapeDtypeStruct(fine_state.shape, F32),
            ),
            in_specs=[anywhere] * 4,
            out_specs=(vmem, vmem),
            scratch_shapes=[
                v((10, 10, 3, 8, L), F32),
                v((F, 4 * CAP * L), F32),
                v((SIDE, 8, 3, 8, L), F32),
                v((SIDE, 8, 8, L), F32),
                v((SIDE, 8, 8, L), F32),
                v((3, SIDE, F, 8, L), F32),
                v((3, SIDE, F, 8, L), F32),
                v((SIDE, F, 8, L), F32),
                v((SIDE, SIDE, 8, L), F32),
                v((CAP, 8, L), F32),
                v((CAP, 8, L), F32),
                v((2 * CAP, 4, 8, L), F32),
                v((2 * CAP, 4, 8, L), F32),
                v((CAP, 4, 8, L), F32),
                v((3, 2 * CAP * 32, L), F32),
                v((n_gy, 5, 8, L), F32),
                v((n_gy, 5, 8, L), F32),
                v((n_gy, 8, L), F32),
                v((n_gy, 8, L), F32),
                v((L, L), BF16),
                v((L, 3 * L), BF16),
                v((3 * L, L), BF16),
                v((L, L), BF16),
                v((L, L), BF16),
                v((L, L), BF16),
                v((4, CAP * 32, L), F32),
                v((2, CAP * 32, L), F32),
                pltpu.SMEM((CAP, n_gy), jnp.int32),
                pltpu.SMEM((CAP, n_gy), jnp.int32),
                pltpu.SMEM((n_gy,), jnp.int32),
                pltpu.SMEM((n_gy,), jnp.int32),
                pltpu.SemaphoreType.DMA((3,)),
                pltpu.SemaphoreType.DMA,
                pltpu.SemaphoreType.DMA((2,)),
                pltpu.SemaphoreType.DMA((3, 4)),
                pltpu.SemaphoreType.DMA((3, 4)),
                pltpu.SemaphoreType.DMA((2,)),
                pltpu.SemaphoreType.DMA((2,)),
            ],
            compiler_params=pltpu.CompilerParams(
                collective_id=0, has_side_effects=True, vmem_limit_bytes=48 * 2**20
            ),
        )(coarse, fine_state, source, live)
        return jnp.transpose(coarse_out, (2, 0, 1, 3)), fine_out

    return jax.shard_map(
        local,
        mesh=mesh,
        in_specs=(P(None, "gx", "gy", None), P(None, ("gx", "gy")), P(), P()),
        out_specs=(P(None, "gx", "gy", None), P(None, ("gx", "gy"))),
        check_vma=False,
    )
```

```python
import jax
import jax.numpy as jnp
from jax import lax
from jax.experimental import pallas as pl
from jax.experimental.pallas import tpu as pltpu
from jax.sharding import PartitionSpec as P

F = 7
CAP = 4
SIDE = 6
L = 128
F32 = jnp.float32
BF16 = jnp.bfloat16
MESH = pl.DeviceIdType.MESH


def iota(shape, dim):
    return lax.broadcasted_iota(jnp.int32, shape, dim)


def take(ref, start, count, stride):
    return ref.reshape(ref.size // L, L)[pl.ds(start, count, stride=stride), :]


def put(ref, start, count, stride, value):
    ref.reshape(ref.size // L, L)[pl.ds(start, count, stride=stride), :] = value


def exact_dot(a, e):
    hi = a.astype(BF16)
    rest = a - hi.astype(F32)
    mid = rest.astype(BF16)
    low = (rest - mid.astype(F32)).astype(BF16)
    out = jnp.dot(hi, e, preferred_element_type=F32)
    out = out + jnp.dot(mid, e, preferred_element_type=F32)
    return out + jnp.dot(low, e, preferred_element_type=F32)


def minmod(a, b):
    return jnp.maximum(jnp.minimum(a, b), 0.0) + jnp.minimum(jnp.maximum(a, b), 0.0)


def half_flux(u, d):
    inv = 1.0 / u[0]
    kk = u[1] * u[1] + u[2] * u[2] + u[3] * u[3]
    p = 0.4 * u[4] - 0.2 * (kk * inv)
    scaled = 0.025 * u[1 + d]
    v = scaled * inv
    out = [scaled]
    for i in range(3):
        term = u[1 + i] * v
        if i == d:
            term = term + 0.025 * p
        out.append(term)
    out += [(u[4] + p) * v, u[5] * v, u[6] * v]
    return out


def split_flux(um, u, up, d):
    h = [0.5 * minmod(c - m, q - c) for m, c, q in zip(um, u, up)]
    left = [c + s for c, s in zip(u, h)]
    right = [c - s for c, s in zip(u, h)]
    plus = [f + 0.1 * c for f, c in zip(half_flux(left, d), left)]
    minus = [f - 0.1 * c for f, c in zip(half_flux(right, d), right)]
    return plus, minus


def react(u, change, t):
    burned = (10.0 * t) * u[5]
    new = [c - g for c, g in zip(u, change)]
    new[4] = new[4] + 2.0 * burned
    new[5] = new[5] - burned
    new[6] = new[6] + burned
    return new


def make_kernel(n_gx, n_gy):
    def kernel(
        coarse, fine, source, live, coarse_out, fine_out,
        S, OWN, FIN, BASE, NEWC, PZ, MZ, PX, MX, CH, CM, BB, MO, MN, GL, FS, FT, GG, SB1, RB1, SB2, RB2,
        EZ, EG, WD, WX, E2, E2X, LW, TT, src_s, live_s, kf_s, kg_s,
        in_sem, fin_sem, tab_sem, h_send, h_recv, m_send, m_recv,
    ):
        a = lax.axis_index("gx")
        b = lax.axis_index("gy")
        up_a, dn_a = lax.rem(a + 1, n_gx), lax.rem(a + n_gx - 1, n_gx)
        up_b, dn_b = lax.rem(b + 1, n_gy), lax.rem(b + n_gy - 1, n_gy)

        barrier = pltpu.get_barrier_semaphore()
        for d in (up_a, dn_a):
            pl.semaphore_signal(barrier, inc=1, device_id=(d, b), device_id_type=MESH)

        def partner(i):
            half = lax.div(i + 1, 2)
            return n_gy // 2 + jnp.where(lax.rem(i, 2) == 1, half, -half)

        def greet(i, _):
            pl.semaphore_signal(
                barrier, inc=1, device_id=(a, lax.rem(b + partner(i), n_gy)), device_id_type=MESH
            )
            return 0

        lax.fori_loop(0, n_gy - 1, greet, 0)

        own = []
        for j in range(3):
            lanes = pl.ds(j * L, L)
            own.append(pltpu.make_async_copy(coarse.at[:, :, :, lanes], OWN.at[2:8, 0:SIDE, j, 0:F, :], in_sem.at[0, j]))
        for j in range(3):
            lanes = pl.ds(j * L, L)
            own.append(pltpu.make_async_copy(coarse.at[:, :, :, lanes], S.at[:, 2:8, j, 0:F, :], in_sem.at[1, j]))
        fin_cp = pltpu.make_async_copy(fine, FIN, fin_sem)
        tabs = [
            pltpu.make_async_copy(source.at[a], src_s, tab_sem.at[0]),
            pltpu.make_async_copy(live.at[a], live_s, tab_sem.at[1]),
        ]
        for cp in tabs + own[:1] + [fin_cp] + own[1:]:
            cp.start()

        row = iota((L, L), 0)
        col = iota((L, L), 1)
        c32 = col & 31
        s32 = col >> 5
        zc = jnp.where(
            c32 < 4, 0, jnp.where(c32 < 8, 5, jnp.where(c32 < 12, c32 - 7, jnp.where(c32 < 16, c32 - 11, (c32 & 3) + 1)))
        )
        EZ[...] = (row == 6 * s32 + zc).astype(F32).astype(BF16)
        fy = (col >> 3) & 7
        fz = col & 7
        cz, cy = fz >> 1, fy >> 1
        EG[:, 0:L] = (row == jnp.where(fz < 4, 0, 4) + cy).astype(F32).astype(BF16)
        EG[:, L : 2 * L] = (row == jnp.where(fy < 4, 8, 12) + cz).astype(F32).astype(BF16)
        EG[:, 2 * L : 3 * L] = (row == 16 + cy * 4 + cz).astype(F32).astype(BF16)

        for cp in tabs:
            cp.wait()

        def route(o, carry):
            owner, alive = carry
            d = lax.rem(b + o, n_gy)
            kf = jnp.int32(0)
            kg = jnp.int32(0)
            back = lax.rem(n_gy - o, n_gy)
            own_new, live_new = [], []
            for k in reversed(range(CAP)):
                kf = jnp.where((src_s[k, b] == d) & (live_s[k, b] == 1), k, kf)
                mine = src_s[k, d] == b
                lv = live_s[k, d]
                kg = jnp.where(mine & (lv == 1), k, kg)
                own_new.append(jnp.where(mine, back, owner[k]))
                live_new.append(jnp.where(mine, lv, alive[k]))
            kf_s[o] = kf
            kg_s[o] = kg
            return tuple(reversed(own_new)), tuple(reversed(live_new))

        zeros = (jnp.int32(0),) * CAP
        owner, alive = lax.fori_loop(0, n_gy, route, (zeros, zeros))

        lane = iota((8, L), 1)
        sub = iota((8, L), 0)
        lc = lane & 31
        ls = lane >> 5
        ly = jnp.where(
            lc < 4, lc + 1, jnp.where(lc < 8, lc - 3, jnp.where(lc < 12, 0, jnp.where(lc < 16, 5, ((lc - 16) >> 2) + 1)))
        )
        low16 = lc < 16

        def ghost_messages(tiles, dst):
            BB[...] = exact_dot(tiles.reshape(SIDE * SIDE * 8, L), EZ[...]).reshape(SIDE, SIDE, 8, L)
            merged = []
            for X in range(4):
                acc = BB[X + 1, 0]
                for y in range(1, 6):
                    acc = jnp.where(low16 & (ly == y), BB[X + 1, y], acc)
                if X in (0, 3):
                    for y in range(1, 5):
                        acc = jnp.where(
                            jnp.logical_not(low16) & (ly == y), BB[0 if X == 0 else 5, y], acc
                        )
                merged.append(acc)
            for k in range(CAP):
                acc = None
                for X in range(4):
                    shift = (32 * (X - k)) % L
                    part = merged[X] if shift == 0 else pltpu.roll(merged[X], shift, 1)
                    acc = part if acc is None else jnp.where(ls == X, part, acc)
                dst[k] = acc

        own[0].wait()
        ghost_messages(OWN[2:8, 0:SIDE, 0], MO)
        fin_cp.wait()
        for t in range(4 * CAP):
            FT[t // 4, t % 4, 0:F, :] = FIN[:, t * L : (t + 1) * L]

        def fill1(o, buf):
            buf[o, 0:4] = FT[kf_s[o]]
            buf[o, 4] = MO[kg_s[o]]

        fill1(0, RB1)

        def fill(o, _):
            fill1(o, SB1)
            return 0

        lax.fori_loop(1, n_gy, fill, 0)
        for cp in own[1:]:
            cp.wait()
        pl.semaphore_wait(barrier, n_gy + 1)

        def halo(j):
            copies = []
            for h, (buf, src, dst, dev) in enumerate(
                (
                    (OWN, OWN.at[6:8, 0:SIDE, j, 0:F, :], OWN.at[0:2, 0:SIDE, j, 0:F, :], (up_a, b)),
                    (OWN, OWN.at[2:4, 0:SIDE, j, 0:F, :], OWN.at[8:10, 0:SIDE, j, 0:F, :], (dn_a, b)),
                    (S, S.at[:, 6:8, j, 0:F, :], S.at[:, 0:2, j, 0:F, :], (a, up_b)),
                    (S, S.at[:, 2:4, j, 0:F, :], S.at[:, 8:10, j, 0:F, :], (a, dn_b)),
                )
            ):
                cp = pltpu.make_async_remote_copy(
                    src_ref=src,
                    dst_ref=dst,
                    send_sem=h_send.at[j, h],
                    recv_sem=h_recv.at[j, h],
                    device_id=dev,
                    device_id_type=MESH,
                )
                cp.start()
                copies.append(cp)
            return copies

        halos = halo(0)

        def send1(i, _):
            o = partner(i)
            pltpu.make_async_remote_copy(
                src_ref=SB1.at[o, :, 0:F, :],
                dst_ref=RB1.at[o, :, 0:F, :],
                send_sem=m_send.at[0],
                recv_sem=m_recv.at[0],
                device_id=(a, lax.rem(b + o, n_gy)),
                device_id_type=MESH,
            ).start()
            return 0

        lax.fori_loop(0, n_gy - 1, send1, 0)
        halos += halo(1) + halo(2)

        def cells(x, j):
            start = ((x + 2) * 24 + j) * 8
            return [take(OWN, start + f, 8, 24) for f in range(F)]

        def y_cells(x, y, j):
            start = ((x * 10 + y + 2) * 3 + j) * 8
            return [take(S, start + f, 8, 24) for f in range(F)]

        def x_split(x, j):
            return split_flux(cells(x - 1, j), cells(x, j), cells(x + 1, j), 0)

        def z_parts(j, _):
            jm, jp = lax.rem(j + 2, 3), lax.rem(j + 1, 3)
            for x in range(SIDE):
                mid = cells(x, j)
                um = [pltpu.roll(jnp.where(lane == L - 1, l, c), 1, 1) for l, c in zip(cells(x, jm), mid)]
                up = [pltpu.roll(jnp.where(lane == 0, r, c), L - 1, 1) for r, c in zip(cells(x, jp), mid)]
                plus, minus = split_flux(um, mid, up, 2)
                for f in range(F):
                    PZ[j, x, f] = plus[f]
                    MZ[j, x, f] = minus[f]
            return 0

        lax.fori_loop(0, 3, z_parts, 0)
        for x in range(1, 5):
            plus, minus = x_split(x, 0)
            for f in range(F):
                PX[x, f] = plus[f]
                MX[x, f] = minus[f]

        ry = (row >> 3) & 7
        rz = row & 7
        rzc, ryc = rz >> 1, ry >> 1
        e6 = (c32 * 43) >> 8
        eyv = jnp.where(c32 < 24, e6 + 1, jnp.where(c32 < 28, 0, 5))
        ezv = jnp.where(c32 < 24, c32 - 6 * e6, (c32 & 3) + 1)
        main = c32 < 24
        wa = main & (ezv >= 1) & (ezv <= 4) & (ryc == eyv - 1) & (rzc == ezv - 1)
        wz = main & (ryc == eyv - 1) & (((ezv == 0) & (rz == 0)) | ((ezv == 5) & (rz == 7)))
        wy = (
            jnp.logical_not(main)
            & (rzc == ezv - 1)
            & (((eyv == 0) & (ry == 0)) | ((eyv == 5) & (ry == 7)))
        )
        for i, w in enumerate((wa, wz, wy)):
            WD[i * L : (i + 1) * L, :] = jnp.where(w, 0.125, 0.0).astype(BF16)
        WX[...] = jnp.where((ryc == (c32 >> 2)) & (rzc == (c32 & 3)), 0.125, 0.0).astype(BF16)
        r32 = row & 31
        rs = row >> 5
        r6 = (r32 * 43) >> 8
        rzv = jnp.where(r32 < 24, r32 - 6 * r6, (r32 & 3) + 1)
        E2[...] = (col == 6 * rs + rzv).astype(F32).astype(BF16)
        E2X[...] = (col == 6 * rs + (r32 & 3) + 1).astype(F32).astype(BF16)

        slot24 = (lane >= 6).astype(jnp.int32) + (lane >= 12).astype(jnp.int32) + (lane >= 18).astype(jnp.int32)
        zpos = lane - 6 * slot24
        alive_lane = jnp.where(
            slot24 == 0, alive[0], jnp.where(slot24 == 1, alive[1], jnp.where(slot24 == 2, alive[2], alive[3]))
        )
        live_z = (lane < 24) & (alive_lane == 1)
        zin = live_z & (zpos >= 1) & (zpos <= 4)
        yin = (sub >= 1) & (sub <= 4)
        inner = yin & zin
        y_low, y_high = (sub == 0) & zin, (sub == 5) & zin
        z_low, z_high = yin & live_z & (zpos == 0), yin & live_z & (zpos == 5)

        def y_parts(x, j):
            plus, minus = split_flux(y_cells(x, -2, j), y_cells(x, -1, j), y_cells(x, 0, j), 1)
            g = [p + pltpu.roll(m, 7, 0) for p, m in zip(plus, minus)]
            return g, [pltpu.roll(v, 7, 0) for v in g]

        def z_faces(x, f, j):
            jm, jp = lax.rem(j + 2, 3), lax.rem(j + 1, 3)
            p, m = PZ[j, x, f], MZ[j, x, f]
            upper = p + pltpu.roll(jnp.where(lane == 0, MZ[jp, x, f], m), L - 1, 1)
            lower = m + pltpu.roll(jnp.where(lane == L - 1, PZ[jm, x, f], p), 1, 1)
            return lower, upper

        def store(x, j, new):
            for f in range(F):
                put(BASE, (x * 24 + j) * 8 + f, 8, 24, new[f])

        zero = jnp.int32(0)
        halos[2].wait_recv()
        halos[3].wait_recv()
        for x in range(SIDE):
            y_lo, y_up = y_parts(x, 0)
            for f in range(F):
                z_lo, z_up = z_faces(x, f, zero)
                whole = (y_up[f] - y_lo[f]) + (z_up - z_lo)
                CH[x, f] = whole
                if 1 <= x <= 4:
                    whole = (jnp.where(y_low, 0.0, y_up[f]) - jnp.where(y_high, 0.0, y_lo[f])) + (
                        jnp.where(z_low, 0.0, z_up) - jnp.where(z_high, 0.0, z_lo)
                    )
                CM[x, f] = whole
        halos[0].wait_recv()
        halos[1].wait_recv()
        ends = {x: x_split(x, 0) for x in (-1, 0, 5, 6)}

        def plus_of(x, f):
            return ends[x][0][f] if x in ends else PX[x, f]

        def minus_of(x, f):
            return ends[x][1][f] if x in ends else MX[x, f]

        lower = [plus_of(-1, f) + minus_of(0, f) for f in range(F)]
        for x in range(SIDE):
            upper = [plus_of(x, f) + minus_of(x + 1, f) for f in range(F)]
            new = react(cells(x, 0), [CH[x, f] + (upper[f] - lower[f]) for f in range(F)], 0.05)
            for f in range(F):
                put(NEWC, x * 64 + f, 8, 8, new[f])
                up_m, lo_m = upper[f], lower[f]
                if x == 0:
                    up_m = jnp.where(inner, 0.0, up_m)
                elif x == 5:
                    lo_m = jnp.where(inner, 0.0, lo_m)
                CM[x, f] = CM[x, f] + (up_m - lo_m)
            lower = upper

        ghost_messages(NEWC[:, 0:SIDE], MN)
        RB2[0] = MN[kg_s[0]]

        def send2(i, _):
            o = partner(i)
            SB2[o] = MN[kg_s[o]]
            pltpu.make_async_remote_copy(
                src_ref=SB2.at[o, 0:F, :],
                dst_ref=RB2.at[o, 0:F, :],
                send_sem=m_send.at[1],
                recv_sem=m_recv.at[1],
                device_id=(a, lax.rem(b + o, n_gy)),
                device_id_type=MESH,
            ).start()
            return 0

        lax.fori_loop(0, n_gy - 1, send2, 0)

        for x in range(SIDE):
            store(x, zero, react(cells(x, 0), [CM[x, f] for f in range(F)], 0.05))
        for cp in halos[4:]:
            cp.wait_recv()

        def rest(j, _):
            before = x_split(-1, j)[0]
            lower = None
            for x in range(SIDE + 1):
                plus, minus = x_split(x, j)
                upper = [p + m for p, m in zip(before, minus)]
                if lower is not None:
                    y_lo, y_up = y_parts(x - 1, j)
                    change = []
                    for f in range(F):
                        z_lo, z_up = z_faces(x - 1, f, j)
                        change.append((upper[f] - lower[f]) + (y_up[f] - y_lo[f]) + (z_up - z_lo))
                    store(x - 1, j, react(cells(x - 1, j), change, 0.05))
                before, lower = plus, upper
            return 0

        lax.fori_loop(1, 3, rest, 0)
        for x in range(SIDE):
            for y in range(SIDE):
                for j in (1, 2):
                    coarse_out[x, y, :, j * L : (j + 1) * L] = BASE[x, y, j, 0:F]

        def wait_messages(whole, sem):
            pltpu.make_async_copy(whole, whole, sem).wait()

        my_src = [lax.rem(b + n_gy - src_s[k, b], n_gy) for k in range(CAP)]
        my_live = [live_s[k, b] for k in range(CAP)]

        def ghost_fields(messages):
            n = len(messages)
            for k in range(n):
                for X in range(4):
                    tile = messages[k]
                    GL[k, X] = tile if X == 0 else pltpu.roll(tile, L - 32 * X, 1)
            expanded = exact_dot(GL[0:n].reshape(n * 32, L), EG[...])
            for i in range(3):
                GG[i, 0 : n * 32] = expanded[:, i * L : (i + 1) * L]
            return [[GG[i, pl.ds(f, 4 * n, stride=8), :] for f in range(F)] for i in range(3)]

        def lane_down(step):
            return lambda v: pltpu.roll(v, step, 1)

        def lane_up(step):
            return lambda v: pltpu.roll(v, L - step, 1)

        def substep(u, ghosts):
            R = u[0].shape[0]
            flane = iota((R, L), 1)
            frow = iota((R, L), 0) & 3
            z, y, odd = flane & 7, (flane >> 3) & 7, (flane >> 6) == 1
            even = jnp.logical_not(odd)

            def x_down(v):
                r = pltpu.roll(v, 64, 1)
                return jnp.where(odd, r, pltpu.roll(r, 1, 0))

            def x_up(v):
                r = pltpu.roll(v, 64, 1)
                return jnp.where(odd, pltpu.roll(r, R - 1, 0), r)

            plan = (
                (2, 0, lane_down(1), lane_up(1), z == 0, z == 7, z < 4),
                (1, 1, lane_down(8), lane_up(8), y == 0, y == 7, y < 4),
                (0, 2, x_down, x_up, (frow == 0) & even, (frow == 3) & odd, even),
            )
            change = None
            faces = []
            for d, gi, down, upw, at_lo, at_hi, lo_side in plan:
                g = ghosts[gi]
                um = [jnp.where(at_lo, w, down(c)) for c, w in zip(u, g)]
                up = [jnp.where(at_hi, w, upw(c)) for c, w in zip(u, g)]
                plus, minus = split_flux(um, u, up, d)
                sign = jnp.where(lo_side, 0.1, -0.1)
                edge = [h + sign * c for h, c in zip(half_flux(g, d), g)]
                lower, upper = [], []
                for f in range(F):
                    lower.append(minus[f] + jnp.where(at_lo, edge[f], down(plus[f])))
                    upper.append(plus[f] + jnp.where(at_hi, edge[f], upw(minus[f])))
                diff = [q - p for q, p in zip(upper, lower)]
                change = diff if change is None else [c + v for c, v in zip(change, diff)]
                faces.append(
                    [
                        jnp.where(at_lo[0:16], -p[0:16], jnp.where(at_hi[0:16], q[0:16], 0.0))
                        for q, p in zip(upper, lower)
                    ]
                )
            return react(u, change, 0.025), faces

        wait_messages(RB1.at[1:n_gy, :, 0:F, :], m_recv.at[0])
        for k in range(CAP):
            FS[k] = RB1[owner[k], 0:4]
            FS[CAP + k] = FT[k]
        old = [MO[k] for k in range(CAP)] + [RB1[my_src[k], 4] for k in range(CAP)]
        u0 = [take(FS, f, 8 * CAP, 8) for f in range(F)]
        u1, faces1 = substep(u0, ghost_fields(old))
        for f in range(F):
            put(FS, f, 8 * CAP, 8, u1[f])
            for i in range(3):
                LW[1 + i, pl.ds(f, 16, stride=8), :] = faces1[i][f]

        mean = [0.5 * (MO[k] + MN[k]) for k in range(CAP)]
        u1 = [take(FS, f, 16, 8) for f in range(F)]
        u2, faces2 = substep(u1, ghost_fields(mean))
        for f in range(F):
            rows = pl.ds(f, 16, stride=8)
            LW[0, rows, :] = u2[f]
            for i in range(3):
                LW[1 + i, rows, :] = LW[1 + i, rows, :] + faces2[i][f]

        TT[0] = exact_dot(jnp.concatenate([LW[0], LW[1], LW[2]], axis=1), WD[...])
        TT[1] = exact_dot(LW[3], WX[...])
        slot_live = jnp.where(ls == 0, alive[0], jnp.where(ls == 1, alive[1], jnp.where(ls == 2, alive[2], alive[3])))
        keep = slot_live == 1

        def by_slot(i, X):
            acc = TT[i, pl.ds(X * 8, 8), :]
            for k in range(1, CAP):
                acc = jnp.where(ls == k, TT[i, pl.ds((k * 4 + X) * 8, 8), :], acc)
            return jnp.where(keep, acc, 0.0)

        l6 = (lc * 43) >> 8
        lyv = jnp.where(lc < 24, l6 + 1, jnp.where(lc < 28, 0, 5))
        blocks = []
        for X in range(4):
            t = by_slot(0, X)
            for y in range(6):
                blocks.append(jnp.where(lyv == y, t, 0.0))
        inside = exact_dot(jnp.concatenate(blocks, axis=0), E2[...])
        lxy = (lc >> 2) + 1
        blocks = []
        for X in (0, 3):
            t = by_slot(1, X)
            for y in range(1, 5):
                blocks.append(jnp.where(lxy == y, t, 0.0))
        across = exact_dot(jnp.concatenate(blocks, axis=0), E2X[...])
        for x in range(SIDE):
            for y in range(SIDE):
                tile = BASE[x, y, 0]
                if 1 <= x <= 4:
                    i = ((x - 1) * 6 + y) * 8
                    part = inside[i : i + 8]
                    if 1 <= y <= 4:
                        tile = jnp.where(zin, part, tile + part)
                    else:
                        tile = tile + part
                elif 1 <= y <= 4:
                    i = ((0 if x == 0 else 4) + y - 1) * 8
                    tile = tile + across[i : i + 8]
                coarse_out[x, y, :, 0:L] = tile[0:F]

        wait_messages(RB2.at[1:n_gy, 0:F, :], m_recv.at[1])
        mean = [0.5 * (RB1[my_src[k], 4] + RB2[my_src[k]]) for k in range(CAP)]
        u1 = [take(FS, CAP * 32 + f, 16, 8) for f in range(F)]
        u2, _ = substep(u1, ghost_fields(mean))
        for f in range(F):
            put(FS, CAP * 32 + f, 16, 8, u2[f])
        for t in range(4 * CAP):
            k = t // 4
            fine_out[:, t * L : (t + 1) * L] = jnp.where(
                my_live[k] == 1, FS[CAP + k, t % 4, 0:F, :], FT[k, t % 4, 0:F, :]
            )

        for cp in halos:
            cp.wait_send()
        wait_messages(SB1.at[1:n_gy, :, 0:F, :], m_send.at[0])
        wait_messages(SB2.at[1:n_gy, 0:F, :], m_send.at[1])

    return kernel


def hand_over(coarse, fine, coarse_out, fine_out, sem):
    copies = [
        pltpu.make_async_copy(coarse, coarse_out, sem.at[0]),
        pltpu.make_async_copy(fine, fine_out, sem.at[1]),
    ]
    for cp in copies:
        cp.start()
    for cp in copies:
        cp.wait()


def solution(mesh):
    n_gx, n_gy = mesh.shape["gx"], mesh.shape["gy"]
    kernel = make_kernel(n_gx, n_gy)

    def local(coarse_state, fine_state, patch_source, patch_live):
        coarse = jnp.transpose(coarse_state, (1, 2, 0, 3))
        source = jnp.transpose(patch_source, (0, 2, 1))
        live = jnp.transpose(patch_live, (0, 2, 1))
        coarse, fine, source, live = (
            pltpu.with_memory_space_constraint(v, pltpu.HBM) for v in (coarse, fine_state, source, live)
        )
        v = pltpu.VMEM
        hbm = pl.BlockSpec(memory_space=pltpu.HBM)
        vmem = pl.BlockSpec(memory_space=pltpu.VMEM)
        coarse_out, fine_out = pl.pallas_call(
            kernel,
            out_shape=(
                pltpu.VMEM(coarse.shape, F32),
                pltpu.VMEM(fine_state.shape, F32),
            ),
            in_specs=[hbm] * 4,
            out_specs=(vmem, vmem),
            scratch_shapes=[
                v((SIDE, 10, 3, 8, L), F32),
                v((10, 8, 3, 8, L), F32),
                v((F, 4 * CAP * L), F32),
                v((SIDE, 8, 3, 8, L), F32),
                v((SIDE, 8, 8, L), F32),
                v((3, SIDE, F, 8, L), F32),
                v((3, SIDE, F, 8, L), F32),
                v((SIDE, F, 8, L), F32),
                v((SIDE, F, 8, L), F32),
                v((SIDE, F, 8, L), F32),
                v((SIDE, F, 8, L), F32),
                v((SIDE, SIDE, 8, L), F32),
                v((CAP, 8, L), F32),
                v((CAP, 8, L), F32),
                v((2 * CAP, 4, 8, L), F32),
                v((2 * CAP, 4, 8, L), F32),
                v((CAP, 4, 8, L), F32),
                v((3, 2 * CAP * 32, L), F32),
                v((n_gy, 5, 8, L), F32),
                v((n_gy, 5, 8, L), F32),
                v((n_gy, 8, L), F32),
                v((n_gy, 8, L), F32),
                v((L, L), BF16),
                v((L, 3 * L), BF16),
                v((3 * L, L), BF16),
                v((L, L), BF16),
                v((L, L), BF16),
                v((L, L), BF16),
                v((4, CAP * 32, L), F32),
                v((2, CAP * 32, L), F32),
                pltpu.SMEM((CAP, n_gy), jnp.int32),
                pltpu.SMEM((CAP, n_gy), jnp.int32),
                pltpu.SMEM((n_gy,), jnp.int32),
                pltpu.SMEM((n_gy,), jnp.int32),
                pltpu.SemaphoreType.DMA((2, 3)),
                pltpu.SemaphoreType.DMA,
                pltpu.SemaphoreType.DMA((2,)),
                pltpu.SemaphoreType.DMA((3, 4)),
                pltpu.SemaphoreType.DMA((3, 4)),
                pltpu.SemaphoreType.DMA((2,)),
                pltpu.SemaphoreType.DMA((2,)),
            ],
            compiler_params=pltpu.CompilerParams(
                collective_id=0, has_side_effects=True, vmem_limit_bytes=48 * 2**20
            ),
        )(coarse, fine, source, live)
        coarse_out, fine_out = (
            pltpu.with_memory_space_constraint(v, pltpu.VMEM) for v in (coarse_out, fine_out)
        )
        coarse_out, fine_out = pl.pallas_call(
            hand_over,
            out_shape=(
                jax.ShapeDtypeStruct(coarse.shape, F32),
                jax.ShapeDtypeStruct(fine_state.shape, F32),
            ),
            in_specs=[vmem] * 2,
            out_specs=(hbm, hbm),
            scratch_shapes=[pltpu.SemaphoreType.DMA((2,))],
        )(coarse_out, fine_out)
        return jnp.transpose(coarse_out, (2, 0, 1, 3)), fine_out

    return jax.shard_map(
        local,
        mesh=mesh,
        in_specs=(P(None, "gx", "gy", None), P(None, ("gx", "gy")), P(), P()),
        out_specs=(P(None, "gx", "gy", None), P(None, ("gx", "gy"))),
        check_vma=False,
    )
```

```python
import jax
import jax.numpy as jnp
from jax import lax
from jax.experimental import pallas as pl
from jax.experimental.pallas import tpu as pltpu
from jax.sharding import PartitionSpec as P

F = 7
CAP = 4
SIDE = 6
L = 128
F32 = jnp.float32
BF16 = jnp.bfloat16
MESH = pl.DeviceIdType.MESH


def iota(shape, dim):
    return lax.broadcasted_iota(jnp.int32, shape, dim)


def take(ref, start, count, stride):
    return ref.reshape(ref.size // L, L)[pl.ds(start, count, stride=stride), :]


def put(ref, start, count, stride, value):
    ref.reshape(ref.size // L, L)[pl.ds(start, count, stride=stride), :] = value


def exact_dot(a, e):
    hi = a.astype(BF16)
    rest = a - hi.astype(F32)
    mid = rest.astype(BF16)
    low = (rest - mid.astype(F32)).astype(BF16)
    out = jnp.dot(hi, e, preferred_element_type=F32)
    out = out + jnp.dot(mid, e, preferred_element_type=F32)
    return out + jnp.dot(low, e, preferred_element_type=F32)


def pick(tile, index):
    return jnp.take_along_axis(tile, index, axis=1, mode="promise_in_bounds")


def minmod(a, b):
    return jnp.maximum(jnp.minimum(a, b), 0.0) + jnp.minimum(jnp.maximum(a, b), 0.0)


def half_flux(u, d):
    inv = 1.0 / u[0]
    kk = u[1] * u[1] + u[2] * u[2] + u[3] * u[3]
    p = 0.4 * u[4] - 0.2 * (kk * inv)
    scaled = 0.025 * u[1 + d]
    v = scaled * inv
    out = [scaled]
    for i in range(3):
        term = u[1 + i] * v
        if i == d:
            term = term + 0.025 * p
        out.append(term)
    out += [(u[4] + p) * v, u[5] * v, u[6] * v]
    return out


def split_flux(um, u, up, d):
    h = [0.5 * minmod(c - m, q - c) for m, c, q in zip(um, u, up)]
    left = [c + s for c, s in zip(u, h)]
    right = [c - s for c, s in zip(u, h)]
    plus = [f + 0.1 * c for f, c in zip(half_flux(left, d), left)]
    minus = [f - 0.1 * c for f, c in zip(half_flux(right, d), right)]
    return plus, minus


def react(u, change, t):
    burned = (10.0 * t) * u[5]
    new = [c - g for c, g in zip(u, change)]
    new[4] = new[4] + 2.0 * burned
    new[5] = new[5] - burned
    new[6] = new[6] + burned
    return new


def make_kernel(n_gx, n_gy):
    def kernel(
        coarse, fine, source, live, coarse_out, fine_out,
        S, OWN, FIN, BASE, NEWC, PZ, MZ, PX, MX, CH, CM, CX, MO, MN, FS, FT, GG, SB0, RB0, SB1, RB1, SB2, RB2,
        WD, WX, LW, TT, src_s, live_s, kf_s, kg_s,
        in_sem, fin_sem, tab_sem, h_send, h_recv, m_send, m_recv,
    ):
        a = lax.axis_index("gx")
        b = lax.axis_index("gy")
        up_a, dn_a = lax.rem(a + 1, n_gx), lax.rem(a + n_gx - 1, n_gx)
        up_b, dn_b = lax.rem(b + 1, n_gy), lax.rem(b + n_gy - 1, n_gy)

        barrier = pltpu.get_barrier_semaphore()
        for d in (up_a, dn_a):
            pl.semaphore_signal(barrier, inc=1, device_id=(d, b), device_id_type=MESH)

        def partner(i):
            half = lax.div(i + 1, 2)
            return n_gy // 2 + jnp.where(lax.rem(i, 2) == 1, half, -half)

        def greet(i, _):
            pl.semaphore_signal(
                barrier, inc=1, device_id=(a, lax.rem(b + partner(i), n_gy)), device_id_type=MESH
            )
            return 0

        lax.fori_loop(0, n_gy - 1, greet, 0)

        own = []
        for j in range(3):
            lanes = pl.ds(j * L, L)
            own.append(pltpu.make_async_copy(coarse.at[:, :, :, lanes], OWN.at[2:8, 0:SIDE, j, 0:F, :], in_sem.at[0, j]))
        for j in range(3):
            lanes = pl.ds(j * L, L)
            own.append(pltpu.make_async_copy(coarse.at[:, :, :, lanes], S.at[:, 2:8, j, 0:F, :], in_sem.at[1, j]))
        fin_cp = pltpu.make_async_copy(fine, FIN, fin_sem)
        tabs = [
            pltpu.make_async_copy(source.at[a], src_s, tab_sem.at[0]),
            pltpu.make_async_copy(live.at[a], live_s, tab_sem.at[1]),
        ]
        for cp in tabs + own[:1] + [fin_cp] + own[1:]:
            cp.start()

        for cp in tabs:
            cp.wait()

        def route(o, carry):
            owner, alive = carry
            d = lax.rem(b + o, n_gy)
            kf = jnp.int32(0)
            kg = jnp.int32(0)
            back = lax.rem(n_gy - o, n_gy)
            own_new, live_new = [], []
            for k in reversed(range(CAP)):
                kf = jnp.where((src_s[k, b] == d) & (live_s[k, b] == 1), k, kf)
                mine = src_s[k, d] == b
                lv = live_s[k, d]
                kg = jnp.where(mine & (lv == 1), k, kg)
                own_new.append(jnp.where(mine, back, owner[k]))
                live_new.append(jnp.where(mine, lv, alive[k]))
            kf_s[o] = kf
            kg_s[o] = kg
            return tuple(reversed(own_new)), tuple(reversed(live_new))

        zeros = (jnp.int32(0),) * CAP
        owner, alive = lax.fori_loop(0, n_gy, route, (zeros, zeros))

        lane = iota((8, L), 1)
        sub = iota((8, L), 0)
        lc = lane & 31
        ls = lane >> 5
        ly = jnp.where(
            lc < 4, lc + 1, jnp.where(lc < 8, lc - 3, jnp.where(lc < 12, 0, jnp.where(lc < 16, 5, ((lc - 16) >> 2) + 1)))
        )
        low16 = lc < 16

        lzc = jnp.where(
            lc < 4, 0, jnp.where(lc < 8, 5, jnp.where(lc < 12, lc - 7, jnp.where(lc < 16, lc - 11, (lc & 3) + 1)))
        )
        to_code = 6 * ls + lzc

        def merge(tile, X):
            acc = pick(tile(X + 1, 0), to_code)
            for y in range(1, 6):
                acc = jnp.where(low16 & (ly == y), pick(tile(X + 1, y), to_code), acc)
            if X in (0, 3):
                for y in range(1, 5):
                    part = pick(tile(0 if X == 0 else 5, y), to_code)
                    acc = jnp.where(jnp.logical_not(low16) & (ly == y), part, acc)
            return acc

        def ghost_messages(merged, dst):
            for k in range(CAP):
                acc = None
                for X in range(4):
                    shift = (32 * (X - k)) % L
                    part = merged[X] if shift == 0 else pltpu.roll(merged[X], shift, 1)
                    acc = part if acc is None else jnp.where(ls == X, part, acc)
                dst[k] = acc

        own[0].wait()
        ghost_messages([merge(lambda x, y: OWN[x + 2, y, 0], X) for X in range(4)], MO)
        fin_cp.wait()
        for t in range(4 * CAP):
            FT[t // 4, t % 4, 0:F, :] = FIN[:, t * L : (t + 1) * L]

        RB0[0] = MO[kg_s[0]]
        RB1[0] = FT[kf_s[0]]

        def fill(o, _):
            SB0[o] = MO[kg_s[o]]
            SB1[o] = FT[kf_s[o]]
            return 0

        lax.fori_loop(1, n_gy, fill, 0)
        for cp in own[1:]:
            cp.wait()
        pl.semaphore_wait(barrier, n_gy + 1)

        def halo(lo, hi, sides=(0, 1, 2, 3)):
            copies = []
            for h, (buf, src, dst, dev) in enumerate(
                (
                    (OWN, OWN.at[6:8, 0:SIDE, lo:hi, 0:F, :], OWN.at[0:2, 0:SIDE, lo:hi, 0:F, :], (up_a, b)),
                    (OWN, OWN.at[2:4, 0:SIDE, lo:hi, 0:F, :], OWN.at[8:10, 0:SIDE, lo:hi, 0:F, :], (dn_a, b)),
                    (S, S.at[:, 6:8, lo:hi, 0:F, :], S.at[:, 0:2, lo:hi, 0:F, :], (a, up_b)),
                    (S, S.at[:, 2:4, lo:hi, 0:F, :], S.at[:, 8:10, lo:hi, 0:F, :], (a, dn_b)),
                )
            ):
                if h not in sides:
                    continue
                cp = pltpu.make_async_remote_copy(
                    src_ref=src,
                    dst_ref=dst,
                    send_sem=h_send.at[lo, h],
                    recv_sem=h_recv.at[lo, h],
                    device_id=dev,
                    device_id_type=MESH,
                )
                cp.start()
                copies.append(cp)
            return copies

        halos = halo(0, 1)

        def send_to_partners(src, dst, sem):
            def send(i, _):
                o = partner(i)
                pltpu.make_async_remote_copy(
                    src_ref=src(o),
                    dst_ref=dst(o),
                    send_sem=m_send.at[sem],
                    recv_sem=m_recv.at[sem],
                    device_id=(a, lax.rem(b + o, n_gy)),
                    device_id_type=MESH,
                ).start()
                return 0

            lax.fori_loop(0, n_gy - 1, send, 0)

        send_to_partners(lambda o: SB0.at[o, 0:F, :], lambda o: RB0.at[o, 0:F, :], 0)
        send_to_partners(lambda o: SB1.at[o, :, 0:F, :], lambda o: RB1.at[o, :, 0:F, :], 1)
        halos_x = halo(1, 3, (0, 1))

        def cells(x, j):
            start = ((x + 2) * 24 + j) * 8
            return [take(OWN, start + f, 8, 24) for f in range(F)]

        def y_cells(x, y, j):
            start = ((x * 10 + y + 2) * 3 + j) * 8
            return [take(S, start + f, 8, 24) for f in range(F)]

        def x_split(x, j):
            return split_flux(cells(x - 1, j), cells(x, j), cells(x + 1, j), 0)

        def z_parts(j, _):
            jm, jp = lax.rem(j + 2, 3), lax.rem(j + 1, 3)
            for x in range(SIDE):
                mid = cells(x, j)
                um = [pltpu.roll(jnp.where(lane == L - 1, l, c), 1, 1) for l, c in zip(cells(x, jm), mid)]
                up = [pltpu.roll(jnp.where(lane == 0, r, c), L - 1, 1) for r, c in zip(cells(x, jp), mid)]
                plus, minus = split_flux(um, mid, up, 2)
                for f in range(F):
                    PZ[j, x, f] = plus[f]
                    MZ[j, x, f] = minus[f]
            return 0

        lax.fori_loop(0, 3, z_parts, 0)
        for x in range(1, 5):
            plus, minus = x_split(x, 0)
            for f in range(F):
                PX[x, f] = plus[f]
                MX[x, f] = minus[f]

        row = iota((L, L), 0)
        col = iota((L, L), 1)
        c32 = col & 31
        ry = (row >> 3) & 7
        rz = row & 7
        rzc, ryc = rz >> 1, ry >> 1
        e6 = (c32 * 43) >> 8
        eyv = jnp.where(c32 < 24, e6 + 1, jnp.where(c32 < 28, 0, 5))
        ezv = jnp.where(c32 < 24, c32 - 6 * e6, (c32 & 3) + 1)
        main = c32 < 24
        wa = main & (ezv >= 1) & (ezv <= 4) & (ryc == eyv - 1) & (rzc == ezv - 1)
        wz = main & (ryc == eyv - 1) & (((ezv == 0) & (rz == 0)) | ((ezv == 5) & (rz == 7)))
        wy = (
            jnp.logical_not(main)
            & (rzc == ezv - 1)
            & (((eyv == 0) & (ry == 0)) | ((eyv == 5) & (ry == 7)))
        )
        for i, w in enumerate((wa, wz, wy)):
            WD[i * L : (i + 1) * L, :] = jnp.where(w, 0.125, 0.0).astype(BF16)
        WX[...] = jnp.where((ryc == (c32 >> 2)) & (rzc == (c32 & 3)), 0.125, 0.0).astype(BF16)
        slot24 = (lane >= 6).astype(jnp.int32) + (lane >= 12).astype(jnp.int32) + (lane >= 18).astype(jnp.int32)
        zpos = lane - 6 * slot24
        alive_lane = jnp.where(
            slot24 == 0, alive[0], jnp.where(slot24 == 1, alive[1], jnp.where(slot24 == 2, alive[2], alive[3]))
        )
        live_z = (lane < 24) & (alive_lane == 1)
        zin = live_z & (zpos >= 1) & (zpos <= 4)
        yin = (sub >= 1) & (sub <= 4)
        inner = yin & zin
        y_low, y_high = (sub == 0) & zin, (sub == 5) & zin
        z_low, z_high = yin & live_z & (zpos == 0), yin & live_z & (zpos == 5)

        def y_parts(x, j):
            plus, minus = split_flux(y_cells(x, -2, j), y_cells(x, -1, j), y_cells(x, 0, j), 1)
            g = [p + pltpu.roll(m, 7, 0) for p, m in zip(plus, minus)]
            return g, [pltpu.roll(v, 7, 0) for v in g]

        def z_faces(x, f, j):
            jm, jp = lax.rem(j + 2, 3), lax.rem(j + 1, 3)
            p, m = PZ[j, x, f], MZ[j, x, f]
            upper = p + pltpu.roll(jnp.where(lane == 0, MZ[jp, x, f], m), L - 1, 1)
            lower = m + pltpu.roll(jnp.where(lane == L - 1, PZ[jm, x, f], p), 1, 1)
            return lower, upper

        def store(x, j, new):
            for f in range(F):
                put(BASE, (x * 24 + j) * 8 + f, 8, 24, new[f])

        zero = jnp.int32(0)
        halos[2].wait_recv()
        halos[3].wait_recv()
        for x in range(SIDE):
            y_lo, y_up = y_parts(x, 0)
            for f in range(F):
                z_lo, z_up = z_faces(x, f, zero)
                whole = (y_up[f] - y_lo[f]) + (z_up - z_lo)
                CH[x, f] = whole
                if 1 <= x <= 4:
                    whole = (jnp.where(y_low, 0.0, y_up[f]) - jnp.where(y_high, 0.0, y_lo[f])) + (
                        jnp.where(z_low, 0.0, z_up) - jnp.where(z_high, 0.0, z_lo)
                    )
                CM[x, f] = whole
        def face(plus, minus):
            return [p + m for p, m in zip(plus, minus)]

        def stored(buf, x):
            return [buf[x, f] for f in range(F)]

        def finish(x, lower, upper):
            new = react(cells(x, 0), [CH[x, f] + (upper[f] - lower[f]) for f in range(F)], 0.05)
            for f in range(F):
                put(NEWC, x * 64 + f, 8, 8, new[f])
                up_m, lo_m = upper[f], lower[f]
                if x == 0:
                    up_m = jnp.where(inner, 0.0, up_m)
                elif x == 5:
                    lo_m = jnp.where(inner, 0.0, lo_m)
                CM[x, f] = CM[x, f] + (up_m - lo_m)

        face12 = face(stored(PX, 1), stored(MX, 2))
        face23 = face(stored(PX, 2), stored(MX, 3))
        face34 = face(stored(PX, 3), stored(MX, 4))
        finish(2, face12, face23)
        finish(3, face23, face34)

        def new_tile(x, y):
            return NEWC[x, y]

        mid = [merge(new_tile, 1), merge(new_tile, 2)]
        halos[0].wait_recv()
        plus_m1, _ = x_split(-1, 0)
        plus_0, minus_0 = x_split(0, 0)
        face01 = face(plus_0, stored(MX, 1))
        finish(0, face(plus_m1, minus_0), face01)
        finish(1, face01, face(stored(PX, 1), stored(MX, 2)))
        first = merge(new_tile, 0)
        halos[1].wait_recv()
        plus_5, minus_5 = x_split(5, 0)
        _, minus_6 = x_split(6, 0)
        face45 = face(stored(PX, 4), minus_5)
        finish(4, face(stored(PX, 3), stored(MX, 4)), face45)
        finish(5, face45, face(plus_5, minus_6))
        ghost_messages([first] + mid + [merge(new_tile, 3)], MN)
        RB2[0] = MN[kg_s[0]]
        for o in range(1, n_gy):
            SB2[o] = MN[kg_s[o]]
        send_to_partners(lambda o: SB2.at[o, 0:F, :], lambda o: RB2.at[o, 0:F, :], 2)

        for x in range(SIDE):
            store(x, zero, react(cells(x, 0), [CM[x, f] for f in range(F)], 0.05))
        halos_y = halo(1, 3, (2, 3))
        for cp in halos_x:
            cp.wait_recv()

        def rest_xz(j, _):
            before = x_split(-1, j)[0]
            lower = None
            for x in range(SIDE + 1):
                plus, minus = x_split(x, j)
                upper = face(before, minus)
                if lower is not None:
                    for f in range(F):
                        z_lo, z_up = z_faces(x - 1, f, j)
                        CX[j, x - 1, f] = (upper[f] - lower[f]) + (z_up - z_lo)
                before, lower = plus, upper
            return 0

        lax.fori_loop(1, 3, rest_xz, 0)

        def wait_messages(whole, sem):
            pltpu.make_async_copy(whole, whole, sem).wait()

        my_src = [lax.rem(b + n_gy - src_s[k, b], n_gy) for k in range(CAP)]
        my_live = [live_s[k, b] for k in range(CAP)]

        tz, ty = lane & 7, (lane >> 3) & 7
        to_cell = (
            jnp.where(tz < 4, 0, 4) + (ty >> 1),
            jnp.where(ty < 4, 8, 12) + (tz >> 1),
            16 + (ty >> 1) * 4 + (tz >> 1),
        )

        def ghost_fields(messages):
            n = len(messages)
            for k in range(n):
                for X in range(4):
                    for i in range(3):
                        GG[i, (k * 4 + X) * 8 : (k * 4 + X) * 8 + 8] = pick(messages[k], to_cell[i] + 32 * X)
            return [[GG[i, pl.ds(f, 4 * n, stride=8), :] for f in range(F)] for i in range(3)]

        def lane_down(step):
            return lambda v: pltpu.roll(v, step, 1)

        def lane_up(step):
            return lambda v: pltpu.roll(v, L - step, 1)

        def substep(u, ghosts):
            R = u[0].shape[0]
            flane = iota((R, L), 1)
            frow = iota((R, L), 0) & 3
            z, y, odd = flane & 7, (flane >> 3) & 7, (flane >> 6) == 1
            even = jnp.logical_not(odd)

            def x_down(v):
                r = pltpu.roll(v, 64, 1)
                return jnp.where(odd, r, pltpu.roll(r, 1, 0))

            def x_up(v):
                r = pltpu.roll(v, 64, 1)
                return jnp.where(odd, pltpu.roll(r, R - 1, 0), r)

            plan = (
                (2, 0, lane_down(1), lane_up(1), z == 0, z == 7, z < 4),
                (1, 1, lane_down(8), lane_up(8), y == 0, y == 7, y < 4),
                (0, 2, x_down, x_up, (frow == 0) & even, (frow == 3) & odd, even),
            )
            change = None
            faces = []
            for d, gi, down, upw, at_lo, at_hi, lo_side in plan:
                g = ghosts[gi]
                um = [jnp.where(at_lo, w, down(c)) for c, w in zip(u, g)]
                up = [jnp.where(at_hi, w, upw(c)) for c, w in zip(u, g)]
                plus, minus = split_flux(um, u, up, d)
                sign = jnp.where(lo_side, 0.1, -0.1)
                edge = [h + sign * c for h, c in zip(half_flux(g, d), g)]
                lower, upper = [], []
                for f in range(F):
                    lower.append(minus[f] + jnp.where(at_lo, edge[f], down(plus[f])))
                    upper.append(plus[f] + jnp.where(at_hi, edge[f], upw(minus[f])))
                diff = [q - p for q, p in zip(upper, lower)]
                change = diff if change is None else [c + v for c, v in zip(change, diff)]
                faces.append(
                    [
                        jnp.where(at_lo[0:16], -p[0:16], jnp.where(at_hi[0:16], q[0:16], 0.0))
                        for q, p in zip(upper, lower)
                    ]
                )
            return react(u, change, 0.025), faces

        wait_messages(RB0.at[1:n_gy, 0:F, :], m_recv.at[0])
        for k in range(CAP):
            FS[CAP + k] = FT[k]
        u0 = [take(FS, CAP * 32 + f, 16, 8) for f in range(F)]
        u1, _ = substep(u0, ghost_fields([RB0[my_src[k]] for k in range(CAP)]))
        for f in range(F):
            put(FS, CAP * 32 + f, 16, 8, u1[f])

        tile_old = ghost_fields([MO[k] for k in range(CAP)])
        wait_messages(RB1.at[1:n_gy, :, 0:F, :], m_recv.at[1])
        for k in range(CAP):
            FS[k] = RB1[owner[k]]
        u0 = [take(FS, f, 16, 8) for f in range(F)]
        u1, faces1 = substep(u0, tile_old)
        u2, faces2 = substep(u1, ghost_fields([0.5 * (MO[k] + MN[k]) for k in range(CAP)]))
        for f in range(F):
            rows = pl.ds(f, 16, stride=8)
            LW[0, rows, :] = u2[f]
            for i in range(3):
                LW[1 + i, rows, :] = faces1[i][f] + faces2[i][f]

        TT[0] = exact_dot(jnp.concatenate([LW[0], LW[1], LW[2]], axis=1), WD[...])
        TT[1] = exact_dot(LW[3], WX[...])
        slot_live = jnp.where(ls == 0, alive[0], jnp.where(ls == 1, alive[1], jnp.where(ls == 2, alive[2], alive[3])))
        keep = slot_live == 1

        def by_slot(i, X):
            acc = TT[i, pl.ds(X * 8, 8), :]
            for k in range(1, CAP):
                acc = jnp.where(ls == k, TT[i, pl.ds((k * 4 + X) * 8, 8), :], acc)
            return jnp.where(keep, acc, 0.0)

        z_mid = (lane < 24) & (zpos >= 1) & (zpos <= 4)
        base_code = jnp.where(lane < 24, 32 * slot24, 0)
        tt = [by_slot(0, X) for X in range(4)]
        tx = {0: by_slot(1, 0), 5: by_slot(1, 3)}
        for x in range(SIDE):
            for y in range(SIDE):
                tile = BASE[x, y, 0]
                if 1 <= x <= 4:
                    if 1 <= y <= 4:
                        part = pick(tt[x - 1], base_code + jnp.where(lane < 24, (y - 1) * 6 + zpos, 0))
                        tile = jnp.where(zin, part, jnp.where(lane < 24, tile + part, tile))
                    else:
                        code = (24 if y == 0 else 28) + jnp.where(z_mid, zpos - 1, 0)
                        tile = jnp.where(z_mid, tile + pick(tt[x - 1], base_code + code), tile)
                elif 1 <= y <= 4:
                    code = (y - 1) * 4 + jnp.where(z_mid, zpos - 1, 0)
                    tile = jnp.where(z_mid, tile + pick(tx[x], base_code + code), tile)
                coarse_out[x, y, :, 0:L] = tile[0:F]

        for cp in halos_y:
            cp.wait_recv()

        def rest_y(j, _):
            for x in range(SIDE):
                y_lo, y_up = y_parts(x, j)
                change = [CX[j, x, f] + (y_up[f] - y_lo[f]) for f in range(F)]
                store(x, j, react(cells(x, j), change, 0.05))
            return 0

        lax.fori_loop(1, 3, rest_y, 0)
        for x in range(SIDE):
            for y in range(SIDE):
                for j in (1, 2):
                    coarse_out[x, y, :, j * L : (j + 1) * L] = BASE[x, y, j, 0:F]

        wait_messages(RB2.at[1:n_gy, 0:F, :], m_recv.at[2])
        mean = [0.5 * (RB0[my_src[k]] + RB2[my_src[k]]) for k in range(CAP)]
        u1 = [take(FS, CAP * 32 + f, 16, 8) for f in range(F)]
        u2, _ = substep(u1, ghost_fields(mean))
        for f in range(F):
            put(FS, CAP * 32 + f, 16, 8, u2[f])
        for t in range(4 * CAP):
            k = t // 4
            fine_out[:, t * L : (t + 1) * L] = jnp.where(
                my_live[k] == 1, FS[CAP + k, t % 4, 0:F, :], FT[k, t % 4, 0:F, :]
            )

        for cp in halos + halos_x + halos_y:
            cp.wait_send()
        wait_messages(SB0.at[1:n_gy, 0:F, :], m_send.at[0])
        wait_messages(SB1.at[1:n_gy, :, 0:F, :], m_send.at[1])
        wait_messages(SB2.at[1:n_gy, 0:F, :], m_send.at[2])

    return kernel


def hand_over(coarse, fine, coarse_out, fine_out, sem):
    copies = [
        pltpu.make_async_copy(coarse, coarse_out, sem.at[0]),
        pltpu.make_async_copy(fine, fine_out, sem.at[1]),
    ]
    for cp in copies:
        cp.start()
    for cp in copies:
        cp.wait()


def solution(mesh):
    n_gx, n_gy = mesh.shape["gx"], mesh.shape["gy"]
    kernel = make_kernel(n_gx, n_gy)

    def local(coarse_state, fine_state, patch_source, patch_live):
        coarse = jnp.transpose(coarse_state, (1, 2, 0, 3))
        source = jnp.transpose(patch_source, (0, 2, 1))
        live = jnp.transpose(patch_live, (0, 2, 1))
        coarse, fine, source, live = (
            pltpu.with_memory_space_constraint(v, pltpu.HBM) for v in (coarse, fine_state, source, live)
        )
        v = pltpu.VMEM
        hbm = pl.BlockSpec(memory_space=pltpu.HBM)
        vmem = pl.BlockSpec(memory_space=pltpu.VMEM)
        coarse_out, fine_out = pl.pallas_call(
            kernel,
            out_shape=(
                pltpu.VMEM(coarse.shape, F32),
                pltpu.VMEM(fine_state.shape, F32),
            ),
            in_specs=[hbm] * 4,
            out_specs=(vmem, vmem),
            scratch_shapes=[
                v((SIDE, 10, 3, 8, L), F32),
                v((10, 8, 3, 8, L), F32),
                v((F, 4 * CAP * L), F32),
                v((SIDE, 8, 3, 8, L), F32),
                v((SIDE, 8, 8, L), F32),
                v((3, SIDE, F, 8, L), F32),
                v((3, SIDE, F, 8, L), F32),
                v((SIDE, F, 8, L), F32),
                v((SIDE, F, 8, L), F32),
                v((SIDE, F, 8, L), F32),
                v((SIDE, F, 8, L), F32),
                v((3, SIDE, F, 8, L), F32),
                v((CAP, 8, L), F32),
                v((CAP, 8, L), F32),
                v((2 * CAP, 4, 8, L), F32),
                v((CAP, 4, 8, L), F32),
                v((3, 2 * CAP * 32, L), F32),
                v((n_gy, 8, L), F32),
                v((n_gy, 8, L), F32),
                v((n_gy, 4, 8, L), F32),
                v((n_gy, 4, 8, L), F32),
                v((n_gy, 8, L), F32),
                v((n_gy, 8, L), F32),
                v((3 * L, L), BF16),
                v((L, L), BF16),
                v((4, CAP * 32, L), F32),
                v((2, CAP * 32, L), F32),
                pltpu.SMEM((CAP, n_gy), jnp.int32),
                pltpu.SMEM((CAP, n_gy), jnp.int32),
                pltpu.SMEM((n_gy,), jnp.int32),
                pltpu.SMEM((n_gy,), jnp.int32),
                pltpu.SemaphoreType.DMA((2, 3)),
                pltpu.SemaphoreType.DMA,
                pltpu.SemaphoreType.DMA((2,)),
                pltpu.SemaphoreType.DMA((2, 4)),
                pltpu.SemaphoreType.DMA((2, 4)),
                pltpu.SemaphoreType.DMA((3,)),
                pltpu.SemaphoreType.DMA((3,)),
            ],
            compiler_params=pltpu.CompilerParams(
                collective_id=0, has_side_effects=True, vmem_limit_bytes=48 * 2**20
            ),
        )(coarse, fine, source, live)
        coarse_out, fine_out = (
            pltpu.with_memory_space_constraint(v, pltpu.VMEM) for v in (coarse_out, fine_out)
        )
        coarse_out, fine_out = pl.pallas_call(
            hand_over,
            out_shape=(
                jax.ShapeDtypeStruct(coarse.shape, F32),
                jax.ShapeDtypeStruct(fine_state.shape, F32),
            ),
            in_specs=[vmem] * 2,
            out_specs=(hbm, hbm),
            scratch_shapes=[pltpu.SemaphoreType.DMA((2,))],
        )(coarse_out, fine_out)
        return jnp.transpose(coarse_out, (2, 0, 1, 3)), fine_out

    return jax.shard_map(
        local,
        mesh=mesh,
        in_specs=(P(None, "gx", "gy", None), P(None, ("gx", "gy")), P(), P()),
        out_specs=(P(None, "gx", "gy", None), P(None, ("gx", "gy"))),
        check_vma=False,
    )
```

```python
import jax
import jax.numpy as jnp
from jax import lax
from jax.experimental import pallas as pl
from jax.experimental.pallas import tpu as pltpu
from jax.sharding import PartitionSpec as P

F = 7
CAP = 4
SIDE = 6
L = 128
F32 = jnp.float32
BF16 = jnp.bfloat16
MESH = pl.DeviceIdType.MESH


def iota(shape, dim):
    return lax.broadcasted_iota(jnp.int32, shape, dim)


def take(ref, start, count, stride):
    return ref.reshape(ref.size // L, L)[pl.ds(start, count, stride=stride), :]


def put(ref, start, count, stride, value):
    ref.reshape(ref.size // L, L)[pl.ds(start, count, stride=stride), :] = value


def exact_dot(a, e):
    hi = a.astype(BF16)
    rest = a - hi.astype(F32)
    mid = rest.astype(BF16)
    low = (rest - mid.astype(F32)).astype(BF16)
    out = jnp.dot(hi, e, preferred_element_type=F32)
    out = out + jnp.dot(mid, e, preferred_element_type=F32)
    return out + jnp.dot(low, e, preferred_element_type=F32)


def pick(tile, index):
    return jnp.take_along_axis(tile, index, axis=1, mode="promise_in_bounds")


def minmod(a, b):
    return jnp.maximum(jnp.minimum(a, b), 0.0) + jnp.minimum(jnp.maximum(a, b), 0.0)


def half_flux(u, d):
    inv = 1.0 / u[0]
    kk = u[1] * u[1] + u[2] * u[2] + u[3] * u[3]
    p = 0.4 * u[4] - 0.2 * (kk * inv)
    scaled = 0.025 * u[1 + d]
    v = scaled * inv
    out = [scaled]
    for i in range(3):
        term = u[1 + i] * v
        if i == d:
            term = term + 0.025 * p
        out.append(term)
    out += [(u[4] + p) * v, u[5] * v, u[6] * v]
    return out


def split_flux(um, u, up, d):
    h = [0.5 * minmod(c - m, q - c) for m, c, q in zip(um, u, up)]
    left = [c + s for c, s in zip(u, h)]
    right = [c - s for c, s in zip(u, h)]
    plus = [f + 0.1 * c for f, c in zip(half_flux(left, d), left)]
    minus = [f - 0.1 * c for f, c in zip(half_flux(right, d), right)]
    return plus, minus


def react(u, change, t):
    burned = (10.0 * t) * u[5]
    new = [c - g for c, g in zip(u, change)]
    new[4] = new[4] + 2.0 * burned
    new[5] = new[5] - burned
    new[6] = new[6] + burned
    return new


def make_kernel(n_gx, n_gy):
    def kernel(
        coarse, fine, source, live, coarse_out, fine_out,
        S, OWN, FIN, BASE, NEWC, PZ, MZ, PX, MX, CH, CM, CX, MO, MN, MOP, MNP, FS, FT, GG, SB0, RB0, SB1, RB1, SB2, RB2,
        WD, WX, LW, TT, src_s, live_s, kf_s, kg_s,
        in_sem, fin_sem, tab_sem, h_send, h_recv, m_send, m_recv,
    ):
        a = lax.axis_index("gx")
        b = lax.axis_index("gy")
        up_a, dn_a = lax.rem(a + 1, n_gx), lax.rem(a + n_gx - 1, n_gx)
        up_b, dn_b = lax.rem(b + 1, n_gy), lax.rem(b + n_gy - 1, n_gy)

        barrier = pltpu.get_barrier_semaphore()
        for d in (up_a, dn_a):
            pl.semaphore_signal(barrier, inc=1, device_id=(d, b), device_id_type=MESH)

        def partner(i):
            half = lax.div(i + 1, 2)
            return n_gy // 2 + jnp.where(lax.rem(i, 2) == 1, half, -half)

        def greet(i, _):
            pl.semaphore_signal(
                barrier, inc=1, device_id=(a, lax.rem(b + partner(i), n_gy)), device_id_type=MESH
            )
            return 0

        lax.fori_loop(0, n_gy - 1, greet, 0)

        own = []
        for j in range(3):
            lanes = pl.ds(j * L, L)
            own.append(pltpu.make_async_copy(coarse.at[:, :, :, lanes], OWN.at[2:8, 0:SIDE, j, 0:F, :], in_sem.at[0, j]))
        for j in range(3):
            lanes = pl.ds(j * L, L)
            own.append(pltpu.make_async_copy(coarse.at[:, :, :, lanes], S.at[:, 2:8, j, 0:F, :], in_sem.at[1, j]))
        fin_cp = pltpu.make_async_copy(fine, FIN, fin_sem)
        tabs = [
            pltpu.make_async_copy(source.at[a], src_s, tab_sem.at[0]),
            pltpu.make_async_copy(live.at[a], live_s, tab_sem.at[1]),
        ]
        for cp in tabs + own[:1] + [fin_cp] + own[1:]:
            cp.start()

        for cp in tabs:
            cp.wait()

        def route(o, carry):
            owner, alive = carry
            d = lax.rem(b + o, n_gy)
            kf = jnp.int32(0)
            kg = jnp.int32(0)
            back = lax.rem(n_gy - o, n_gy)
            own_new, live_new = [], []
            for k in reversed(range(CAP)):
                kf = jnp.where((src_s[k, b] == d) & (live_s[k, b] == 1), k, kf)
                mine = src_s[k, d] == b
                lv = live_s[k, d]
                kg = jnp.where(mine & (lv == 1), k, kg)
                own_new.append(jnp.where(mine, back, owner[k]))
                live_new.append(jnp.where(mine, lv, alive[k]))
            kf_s[o] = kf
            kg_s[o] = kg
            return tuple(reversed(own_new)), tuple(reversed(live_new))

        zeros = (jnp.int32(0),) * CAP
        owner, alive = lax.fori_loop(0, n_gy, route, (zeros, zeros))

        lane = iota((8, L), 1)
        sub = iota((8, L), 0)
        lc = lane & 31
        ls = lane >> 5
        ly = jnp.where(
            lc < 4, lc + 1, jnp.where(lc < 8, lc - 3, jnp.where(lc < 12, 0, jnp.where(lc < 16, 5, ((lc - 16) >> 2) + 1)))
        )
        low16 = lc < 16

        lzc = jnp.where(
            lc < 4, 0, jnp.where(lc < 8, 5, jnp.where(lc < 12, lc - 7, jnp.where(lc < 16, lc - 11, (lc & 3) + 1)))
        )
        to_code = 6 * ls + lzc

        def merge(tile, X):
            acc = pick(tile(X + 1, 0), to_code)
            for y in range(1, 6):
                acc = jnp.where(low16 & (ly == y), pick(tile(X + 1, y), to_code), acc)
            if X in (0, 3):
                for y in range(1, 5):
                    part = pick(tile(0 if X == 0 else 5, y), to_code)
                    acc = jnp.where(jnp.logical_not(low16) & (ly == y), part, acc)
            return acc

        hole = (lane >= 48) & (lane < 64)
        from_lane = jnp.where(sub < 3, 16 * sub, jnp.where(sub == 3, 64, 16 * sub + 32))
        to_hole = jnp.where(hole & (sub < 6), from_lane + lane - 48, lane)
        from_hole = 48 + (lane & 15)
        part16 = lane >> 4
        from_row = jnp.where(
            part16 < 3, part16, jnp.where(part16 == 4, 3, jnp.where(part16 >= 6, part16 - 2, 8))
        )

        def pack(tile):
            return jnp.where(hole, pick(jnp.broadcast_to(tile[6:7], (8, L)), to_hole), tile)

        def unpack(tile):
            last = jnp.where(sub == from_row, pick(tile, from_hole), 0.0)
            for step in (4, 2, 1):
                last = last + pltpu.roll(last, step, 0)
            return jnp.where(sub == 6, last, tile)

        def ghost_messages(merged, dst, packed):
            for k in range(CAP):
                acc = None
                for X in range(4):
                    shift = (32 * (X - k)) % L
                    part = merged[X] if shift == 0 else pltpu.roll(merged[X], shift, 1)
                    acc = part if acc is None else jnp.where(ls == X, part, acc)
                dst[k] = acc
                packed[k] = pack(acc)

        own[0].wait()
        ghost_messages([merge(lambda x, y: OWN[x + 2, y, 0], X) for X in range(4)], MO, MOP)
        fin_cp.wait()
        for t in range(4 * CAP):
            FT[t // 4, t % 4, 0:F, :] = FIN[:, t * L : (t + 1) * L]

        RB0[0] = MOP[kg_s[0]]
        RB1[0] = FT[kf_s[0]]

        def fill(o, _):
            SB0[o] = MOP[kg_s[o]]
            SB1[o] = FT[kf_s[o]]
            return 0

        lax.fori_loop(1, n_gy, fill, 0)
        for cp in own[1:]:
            cp.wait()
        pl.semaphore_wait(barrier, n_gy + 1)

        def halo(lo, hi, sides=(0, 1, 2, 3)):
            copies = []
            for h, (buf, src, dst, dev) in enumerate(
                (
                    (OWN, OWN.at[6:8, 0:SIDE, lo:hi, 0:F, :], OWN.at[0:2, 0:SIDE, lo:hi, 0:F, :], (up_a, b)),
                    (OWN, OWN.at[2:4, 0:SIDE, lo:hi, 0:F, :], OWN.at[8:10, 0:SIDE, lo:hi, 0:F, :], (dn_a, b)),
                    (S, S.at[:, 6:8, lo:hi, 0:F, :], S.at[:, 0:2, lo:hi, 0:F, :], (a, up_b)),
                    (S, S.at[:, 2:4, lo:hi, 0:F, :], S.at[:, 8:10, lo:hi, 0:F, :], (a, dn_b)),
                )
            ):
                if h not in sides:
                    continue
                cp = pltpu.make_async_remote_copy(
                    src_ref=src,
                    dst_ref=dst,
                    send_sem=h_send.at[lo, h],
                    recv_sem=h_recv.at[lo, h],
                    device_id=dev,
                    device_id_type=MESH,
                )
                cp.start()
                copies.append(cp)
            return copies

        halos = halo(0, 1)

        def send_to_partners(src, dst, sem):
            def send(i, _):
                o = partner(i)
                pltpu.make_async_remote_copy(
                    src_ref=src(o),
                    dst_ref=dst(o),
                    send_sem=m_send.at[sem],
                    recv_sem=m_recv.at[sem],
                    device_id=(a, lax.rem(b + o, n_gy)),
                    device_id_type=MESH,
                ).start()
                return 0

            lax.fori_loop(0, n_gy - 1, send, 0)

        send_to_partners(lambda o: SB0.at[o, 0 : F - 1, :], lambda o: RB0.at[o, 0 : F - 1, :], 0)
        send_to_partners(lambda o: SB1.at[o, :, 0:F, :], lambda o: RB1.at[o, :, 0:F, :], 1)
        halos_x = halo(1, 3, (0, 1))

        def cells(x, j):
            start = ((x + 2) * 24 + j) * 8
            return [take(OWN, start + f, 8, 24) for f in range(F)]

        def y_cells(x, y, j):
            start = ((x * 10 + y + 2) * 3 + j) * 8
            return [take(S, start + f, 8, 24) for f in range(F)]

        def x_split(x, j):
            return split_flux(cells(x - 1, j), cells(x, j), cells(x + 1, j), 0)

        def z_parts(j, _):
            jm, jp = lax.rem(j + 2, 3), lax.rem(j + 1, 3)
            for x in range(SIDE):
                mid = cells(x, j)
                um = [pltpu.roll(jnp.where(lane == L - 1, l, c), 1, 1) for l, c in zip(cells(x, jm), mid)]
                up = [pltpu.roll(jnp.where(lane == 0, r, c), L - 1, 1) for r, c in zip(cells(x, jp), mid)]
                plus, minus = split_flux(um, mid, up, 2)
                for f in range(F):
                    PZ[j, x, f] = plus[f]
                    MZ[j, x, f] = minus[f]
            return 0

        lax.fori_loop(0, 3, z_parts, 0)
        for x in range(1, 5):
            plus, minus = x_split(x, 0)
            for f in range(F):
                PX[x, f] = plus[f]
                MX[x, f] = minus[f]

        row = iota((L, L), 0)
        col = iota((L, L), 1)
        c32 = col & 31
        ry = (row >> 3) & 7
        rz = row & 7
        rzc, ryc = rz >> 1, ry >> 1
        e6 = (c32 * 43) >> 8
        eyv = jnp.where(c32 < 24, e6 + 1, jnp.where(c32 < 28, 0, 5))
        ezv = jnp.where(c32 < 24, c32 - 6 * e6, (c32 & 3) + 1)
        main = c32 < 24
        wa = main & (ezv >= 1) & (ezv <= 4) & (ryc == eyv - 1) & (rzc == ezv - 1)
        wz = main & (ryc == eyv - 1) & (((ezv == 0) & (rz == 0)) | ((ezv == 5) & (rz == 7)))
        wy = (
            jnp.logical_not(main)
            & (rzc == ezv - 1)
            & (((eyv == 0) & (ry == 0)) | ((eyv == 5) & (ry == 7)))
        )
        for i, w in enumerate((wa, wz, wy)):
            WD[i * L : (i + 1) * L, :] = jnp.where(w, 0.125, 0.0).astype(BF16)
        WX[...] = jnp.where((ryc == (c32 >> 2)) & (rzc == (c32 & 3)), 0.125, 0.0).astype(BF16)
        slot24 = (lane >= 6).astype(jnp.int32) + (lane >= 12).astype(jnp.int32) + (lane >= 18).astype(jnp.int32)
        zpos = lane - 6 * slot24
        alive_lane = jnp.where(
            slot24 == 0, alive[0], jnp.where(slot24 == 1, alive[1], jnp.where(slot24 == 2, alive[2], alive[3]))
        )
        live_z = (lane < 24) & (alive_lane == 1)
        zin = live_z & (zpos >= 1) & (zpos <= 4)
        yin = (sub >= 1) & (sub <= 4)
        inner = yin & zin
        y_low, y_high = (sub == 0) & zin, (sub == 5) & zin
        z_low, z_high = yin & live_z & (zpos == 0), yin & live_z & (zpos == 5)

        def y_parts(x, j):
            plus, minus = split_flux(y_cells(x, -2, j), y_cells(x, -1, j), y_cells(x, 0, j), 1)
            g = [p + pltpu.roll(m, 7, 0) for p, m in zip(plus, minus)]
            return g, [pltpu.roll(v, 7, 0) for v in g]

        def z_faces(x, f, j):
            jm, jp = lax.rem(j + 2, 3), lax.rem(j + 1, 3)
            p, m = PZ[j, x, f], MZ[j, x, f]
            upper = p + pltpu.roll(jnp.where(lane == 0, MZ[jp, x, f], m), L - 1, 1)
            lower = m + pltpu.roll(jnp.where(lane == L - 1, PZ[jm, x, f], p), 1, 1)
            return lower, upper

        def store(x, j, new):
            for f in range(F):
                put(BASE, (x * 24 + j) * 8 + f, 8, 24, new[f])

        zero = jnp.int32(0)
        halos[2].wait_recv()
        halos[3].wait_recv()
        for x in range(SIDE):
            y_lo, y_up = y_parts(x, 0)
            for f in range(F):
                z_lo, z_up = z_faces(x, f, zero)
                whole = (y_up[f] - y_lo[f]) + (z_up - z_lo)
                CH[x, f] = whole
                if 1 <= x <= 4:
                    whole = (jnp.where(y_low, 0.0, y_up[f]) - jnp.where(y_high, 0.0, y_lo[f])) + (
                        jnp.where(z_low, 0.0, z_up) - jnp.where(z_high, 0.0, z_lo)
                    )
                CM[x, f] = whole
        def face(plus, minus):
            return [p + m for p, m in zip(plus, minus)]

        def stored(buf, x):
            return [buf[x, f] for f in range(F)]

        def finish(x, lower, upper):
            new = react(cells(x, 0), [CH[x, f] + (upper[f] - lower[f]) for f in range(F)], 0.05)
            for f in range(F):
                put(NEWC, x * 64 + f, 8, 8, new[f])
                up_m, lo_m = upper[f], lower[f]
                if x == 0:
                    up_m = jnp.where(inner, 0.0, up_m)
                elif x == 5:
                    lo_m = jnp.where(inner, 0.0, lo_m)
                CM[x, f] = CM[x, f] + (up_m - lo_m)

        face12 = face(stored(PX, 1), stored(MX, 2))
        face23 = face(stored(PX, 2), stored(MX, 3))
        face34 = face(stored(PX, 3), stored(MX, 4))
        finish(2, face12, face23)
        finish(3, face23, face34)

        def new_tile(x, y):
            return NEWC[x, y]

        mid = [merge(new_tile, 1), merge(new_tile, 2)]
        halos[0].wait_recv()
        plus_m1, _ = x_split(-1, 0)
        plus_0, minus_0 = x_split(0, 0)
        face01 = face(plus_0, stored(MX, 1))
        finish(0, face(plus_m1, minus_0), face01)
        finish(1, face01, face(stored(PX, 1), stored(MX, 2)))
        first = merge(new_tile, 0)
        halos[1].wait_recv()
        plus_5, minus_5 = x_split(5, 0)
        _, minus_6 = x_split(6, 0)
        face45 = face(stored(PX, 4), minus_5)
        finish(4, face(stored(PX, 3), stored(MX, 4)), face45)
        finish(5, face45, face(plus_5, minus_6))
        ghost_messages([first] + mid + [merge(new_tile, 3)], MN, MNP)
        RB2[0] = MNP[kg_s[0]]
        for o in range(1, n_gy):
            SB2[o] = MNP[kg_s[o]]
        send_to_partners(lambda o: SB2.at[o, 0 : F - 1, :], lambda o: RB2.at[o, 0 : F - 1, :], 2)

        for x in range(SIDE):
            store(x, zero, react(cells(x, 0), [CM[x, f] for f in range(F)], 0.05))
        halos_y = halo(1, 3, (2, 3))
        for cp in halos_x:
            cp.wait_recv()

        def rest_xz(j, _):
            before = x_split(-1, j)[0]
            lower = None
            for x in range(SIDE + 1):
                plus, minus = x_split(x, j)
                upper = face(before, minus)
                if lower is not None:
                    for f in range(F):
                        z_lo, z_up = z_faces(x - 1, f, j)
                        CX[j, x - 1, f] = (upper[f] - lower[f]) + (z_up - z_lo)
                before, lower = plus, upper
            return 0

        lax.fori_loop(1, 3, rest_xz, 0)

        def wait_messages(whole, sem):
            pltpu.make_async_copy(whole, whole, sem).wait()

        my_src = [lax.rem(b + n_gy - src_s[k, b], n_gy) for k in range(CAP)]
        my_live = [live_s[k, b] for k in range(CAP)]

        tz, ty = lane & 7, (lane >> 3) & 7
        to_cell = (
            jnp.where(tz < 4, 0, 4) + (ty >> 1),
            jnp.where(ty < 4, 8, 12) + (tz >> 1),
            16 + (ty >> 1) * 4 + (tz >> 1),
        )

        def ghost_fields(messages):
            n = len(messages)
            for k in range(n):
                for X in range(4):
                    for i in range(3):
                        GG[i, (k * 4 + X) * 8 : (k * 4 + X) * 8 + 8] = pick(messages[k], to_cell[i] + 32 * X)
            return [[GG[i, pl.ds(f, 4 * n, stride=8), :] for f in range(F)] for i in range(3)]

        def lane_down(step):
            return lambda v: pltpu.roll(v, step, 1)

        def lane_up(step):
            return lambda v: pltpu.roll(v, L - step, 1)

        def substep(u, ghosts):
            R = u[0].shape[0]
            flane = iota((R, L), 1)
            frow = iota((R, L), 0) & 3
            z, y, odd = flane & 7, (flane >> 3) & 7, (flane >> 6) == 1
            even = jnp.logical_not(odd)

            def x_down(v):
                r = pltpu.roll(v, 64, 1)
                return jnp.where(odd, r, pltpu.roll(r, 1, 0))

            def x_up(v):
                r = pltpu.roll(v, 64, 1)
                return jnp.where(odd, pltpu.roll(r, R - 1, 0), r)

            plan = (
                (2, 0, lane_down(1), lane_up(1), z == 0, z == 7, z < 4),
                (1, 1, lane_down(8), lane_up(8), y == 0, y == 7, y < 4),
                (0, 2, x_down, x_up, (frow == 0) & even, (frow == 3) & odd, even),
            )
            change = None
            faces = []
            for d, gi, down, upw, at_lo, at_hi, lo_side in plan:
                g = ghosts[gi]
                um = [jnp.where(at_lo, w, down(c)) for c, w in zip(u, g)]
                up = [jnp.where(at_hi, w, upw(c)) for c, w in zip(u, g)]
                plus, minus = split_flux(um, u, up, d)
                sign = jnp.where(lo_side, 0.1, -0.1)
                edge = [h + sign * c for h, c in zip(half_flux(g, d), g)]
                lower, upper = [], []
                for f in range(F):
                    lower.append(minus[f] + jnp.where(at_lo, edge[f], down(plus[f])))
                    upper.append(plus[f] + jnp.where(at_hi, edge[f], upw(minus[f])))
                diff = [q - p for q, p in zip(upper, lower)]
                change = diff if change is None else [c + v for c, v in zip(change, diff)]
                faces.append(
                    [
                        jnp.where(at_lo[0:16], -p[0:16], jnp.where(at_hi[0:16], q[0:16], 0.0))
                        for q, p in zip(upper, lower)
                    ]
                )
            return react(u, change, 0.025), faces

        wait_messages(RB0.at[1:n_gy, 0 : F - 1, :], m_recv.at[0])
        for k in range(CAP):
            FS[CAP + k] = FT[k]
        u0 = [take(FS, CAP * 32 + f, 16, 8) for f in range(F)]
        u1, _ = substep(u0, ghost_fields([unpack(RB0[my_src[k]]) for k in range(CAP)]))
        for f in range(F):
            put(FS, CAP * 32 + f, 16, 8, u1[f])

        tile_old = ghost_fields([MO[k] for k in range(CAP)])
        wait_messages(RB1.at[1:n_gy, :, 0:F, :], m_recv.at[1])
        for k in range(CAP):
            FS[k] = RB1[owner[k]]
        u0 = [take(FS, f, 16, 8) for f in range(F)]
        u1, faces1 = substep(u0, tile_old)
        u2, faces2 = substep(u1, ghost_fields([0.5 * (MO[k] + MN[k]) for k in range(CAP)]))
        for f in range(F):
            rows = pl.ds(f, 16, stride=8)
            LW[0, rows, :] = u2[f]
            for i in range(3):
                LW[1 + i, rows, :] = faces1[i][f] + faces2[i][f]

        TT[0] = exact_dot(jnp.concatenate([LW[0], LW[1], LW[2]], axis=1), WD[...])
        TT[1] = exact_dot(LW[3], WX[...])
        slot_live = jnp.where(ls == 0, alive[0], jnp.where(ls == 1, alive[1], jnp.where(ls == 2, alive[2], alive[3])))
        keep = slot_live == 1

        def by_slot(i, X):
            acc = TT[i, pl.ds(X * 8, 8), :]
            for k in range(1, CAP):
                acc = jnp.where(ls == k, TT[i, pl.ds((k * 4 + X) * 8, 8), :], acc)
            return jnp.where(keep, acc, 0.0)

        z_mid = (lane < 24) & (zpos >= 1) & (zpos <= 4)
        base_code = jnp.where(lane < 24, 32 * slot24, 0)
        tt = [by_slot(0, X) for X in range(4)]
        tx = {0: by_slot(1, 0), 5: by_slot(1, 3)}
        for x in range(SIDE):
            for y in range(SIDE):
                tile = BASE[x, y, 0]
                if 1 <= x <= 4:
                    if 1 <= y <= 4:
                        part = pick(tt[x - 1], base_code + jnp.where(lane < 24, (y - 1) * 6 + zpos, 0))
                        tile = jnp.where(zin, part, jnp.where(lane < 24, tile + part, tile))
                    else:
                        code = (24 if y == 0 else 28) + jnp.where(z_mid, zpos - 1, 0)
                        tile = jnp.where(z_mid, tile + pick(tt[x - 1], base_code + code), tile)
                elif 1 <= y <= 4:
                    code = (y - 1) * 4 + jnp.where(z_mid, zpos - 1, 0)
                    tile = jnp.where(z_mid, tile + pick(tx[x], base_code + code), tile)
                coarse_out[x, y, :, 0:L] = tile[0:F]

        for cp in halos_y:
            cp.wait_recv()

        def rest_y(j, _):
            for x in range(SIDE):
                y_lo, y_up = y_parts(x, j)
                change = [CX[j, x, f] + (y_up[f] - y_lo[f]) for f in range(F)]
                store(x, j, react(cells(x, j), change, 0.05))
            return 0

        lax.fori_loop(1, 3, rest_y, 0)
        for x in range(SIDE):
            for y in range(SIDE):
                for j in (1, 2):
                    coarse_out[x, y, :, j * L : (j + 1) * L] = BASE[x, y, j, 0:F]

        wait_messages(RB2.at[1:n_gy, 0 : F - 1, :], m_recv.at[2])
        mean = [unpack(0.5 * (RB0[my_src[k]] + RB2[my_src[k]])) for k in range(CAP)]
        u1 = [take(FS, CAP * 32 + f, 16, 8) for f in range(F)]
        u2, _ = substep(u1, ghost_fields(mean))
        for f in range(F):
            put(FS, CAP * 32 + f, 16, 8, u2[f])
        for t in range(4 * CAP):
            k = t // 4
            fine_out[:, t * L : (t + 1) * L] = jnp.where(
                my_live[k] == 1, FS[CAP + k, t % 4, 0:F, :], FT[k, t % 4, 0:F, :]
            )

        for cp in halos + halos_x + halos_y:
            cp.wait_send()
        wait_messages(SB0.at[1:n_gy, 0 : F - 1, :], m_send.at[0])
        wait_messages(SB1.at[1:n_gy, :, 0:F, :], m_send.at[1])
        wait_messages(SB2.at[1:n_gy, 0 : F - 1, :], m_send.at[2])

    return kernel


def hand_over(coarse, fine, coarse_out, fine_out, sem):
    copies = [
        pltpu.make_async_copy(coarse, coarse_out, sem.at[0]),
        pltpu.make_async_copy(fine, fine_out, sem.at[1]),
    ]
    for cp in copies:
        cp.start()
    for cp in copies:
        cp.wait()


def solution(mesh):
    n_gx, n_gy = mesh.shape["gx"], mesh.shape["gy"]
    kernel = make_kernel(n_gx, n_gy)

    def local(coarse_state, fine_state, patch_source, patch_live):
        coarse = jnp.transpose(coarse_state, (1, 2, 0, 3))
        source = jnp.transpose(patch_source, (0, 2, 1))
        live = jnp.transpose(patch_live, (0, 2, 1))
        coarse, fine, source, live = (
            pltpu.with_memory_space_constraint(v, pltpu.HBM) for v in (coarse, fine_state, source, live)
        )
        v = pltpu.VMEM
        hbm = pl.BlockSpec(memory_space=pltpu.HBM)
        vmem = pl.BlockSpec(memory_space=pltpu.VMEM)
        coarse_out, fine_out = pl.pallas_call(
            kernel,
            out_shape=(
                pltpu.VMEM(coarse.shape, F32),
                pltpu.VMEM(fine_state.shape, F32),
            ),
            in_specs=[hbm] * 4,
            out_specs=(vmem, vmem),
            scratch_shapes=[
                v((SIDE, 10, 3, 8, L), F32),
                v((10, 8, 3, 8, L), F32),
                v((F, 4 * CAP * L), F32),
                v((SIDE, 8, 3, 8, L), F32),
                v((SIDE, 8, 8, L), F32),
                v((3, SIDE, F, 8, L), F32),
                v((3, SIDE, F, 8, L), F32),
                v((SIDE, F, 8, L), F32),
                v((SIDE, F, 8, L), F32),
                v((SIDE, F, 8, L), F32),
                v((SIDE, F, 8, L), F32),
                v((3, SIDE, F, 8, L), F32),
                v((CAP, 8, L), F32),
                v((CAP, 8, L), F32),
                v((CAP, 8, L), F32),
                v((CAP, 8, L), F32),
                v((2 * CAP, 4, 8, L), F32),
                v((CAP, 4, 8, L), F32),
                v((3, 2 * CAP * 32, L), F32),
                v((n_gy, 8, L), F32),
                v((n_gy, 8, L), F32),
                v((n_gy, 4, 8, L), F32),
                v((n_gy, 4, 8, L), F32),
                v((n_gy, 8, L), F32),
                v((n_gy, 8, L), F32),
                v((3 * L, L), BF16),
                v((L, L), BF16),
                v((4, CAP * 32, L), F32),
                v((2, CAP * 32, L), F32),
                pltpu.SMEM((CAP, n_gy), jnp.int32),
                pltpu.SMEM((CAP, n_gy), jnp.int32),
                pltpu.SMEM((n_gy,), jnp.int32),
                pltpu.SMEM((n_gy,), jnp.int32),
                pltpu.SemaphoreType.DMA((2, 3)),
                pltpu.SemaphoreType.DMA,
                pltpu.SemaphoreType.DMA((2,)),
                pltpu.SemaphoreType.DMA((2, 4)),
                pltpu.SemaphoreType.DMA((2, 4)),
                pltpu.SemaphoreType.DMA((3,)),
                pltpu.SemaphoreType.DMA((3,)),
            ],
            compiler_params=pltpu.CompilerParams(
                collective_id=0, has_side_effects=True, vmem_limit_bytes=48 * 2**20
            ),
        )(coarse, fine, source, live)
        coarse_out, fine_out = (
            pltpu.with_memory_space_constraint(v, pltpu.VMEM) for v in (coarse_out, fine_out)
        )
        coarse_out, fine_out = pl.pallas_call(
            hand_over,
            out_shape=(
                jax.ShapeDtypeStruct(coarse.shape, F32),
                jax.ShapeDtypeStruct(fine_state.shape, F32),
            ),
            in_specs=[vmem] * 2,
            out_specs=(hbm, hbm),
            scratch_shapes=[pltpu.SemaphoreType.DMA((2,))],
        )(coarse_out, fine_out)
        return jnp.transpose(coarse_out, (2, 0, 1, 3)), fine_out

    return jax.shard_map(
        local,
        mesh=mesh,
        in_specs=(P(None, "gx", "gy", None), P(None, ("gx", "gy")), P(), P()),
        out_specs=(P(None, "gx", "gy", None), P(None, ("gx", "gy"))),
        check_vma=False,
    )
```

```python
import jax
import jax.numpy as jnp
from jax import lax
from jax.experimental import pallas as pl
from jax.experimental.pallas import tpu as pltpu
from jax.sharding import PartitionSpec as P

F = 7
CAP = 4
SIDE = 6
L = 128
F32 = jnp.float32
BF16 = jnp.bfloat16
MESH = pl.DeviceIdType.MESH


def iota(shape, dim):
    return lax.broadcasted_iota(jnp.int32, shape, dim)


def take(ref, start, count, stride):
    return ref.reshape(ref.size // L, L)[pl.ds(start, count, stride=stride), :]


def put(ref, start, count, stride, value):
    ref.reshape(ref.size // L, L)[pl.ds(start, count, stride=stride), :] = value


def exact_dot(a, e):
    hi = a.astype(BF16)
    rest = a - hi.astype(F32)
    mid = rest.astype(BF16)
    low = (rest - mid.astype(F32)).astype(BF16)
    out = jnp.dot(hi, e, preferred_element_type=F32)
    out = out + jnp.dot(mid, e, preferred_element_type=F32)
    return out + jnp.dot(low, e, preferred_element_type=F32)


def pick(tile, index):
    return jnp.take_along_axis(tile, index, axis=1, mode="promise_in_bounds")


def minmod(a, b):
    return jnp.maximum(jnp.minimum(a, b), 0.0) + jnp.minimum(jnp.maximum(a, b), 0.0)


def half_flux(u, d):
    inv = 1.0 / u[0]
    kk = u[1] * u[1] + u[2] * u[2] + u[3] * u[3]
    p = 0.4 * u[4] - 0.2 * (kk * inv)
    scaled = 0.025 * u[1 + d]
    v = scaled * inv
    out = [scaled]
    for i in range(3):
        term = u[1 + i] * v
        if i == d:
            term = term + 0.025 * p
        out.append(term)
    out += [(u[4] + p) * v, u[5] * v, u[6] * v]
    return out


def split_flux(um, u, up, d):
    h = [0.5 * minmod(c - m, q - c) for m, c, q in zip(um, u, up)]
    left = [c + s for c, s in zip(u, h)]
    right = [c - s for c, s in zip(u, h)]
    plus = [f + 0.1 * c for f, c in zip(half_flux(left, d), left)]
    minus = [f - 0.1 * c for f, c in zip(half_flux(right, d), right)]
    return plus, minus


def react(u, change, t):
    burned = (10.0 * t) * u[5]
    new = [c - g for c, g in zip(u, change)]
    new[4] = new[4] + 2.0 * burned
    new[5] = new[5] - burned
    new[6] = new[6] + burned
    return new


def make_kernel(n_gx, n_gy):
    def kernel(
        coarse, fine, source, live, coarse_out, fine_out,
        S, OWN, FIN, BASE, NEWC, PZ, MZ, PX, MX, CH, CM, CX, MO, MN, MOP, MNP, FS, FT, GG, SB0, RB0, SB1, RB1, SB2, RB2,
        WD, WX, LW, TT, src_s, live_s, kf_s, kg_s,
        in_sem, fin_sem, tab_sem, h_send, h_recv, m_send, m_recv,
    ):
        a = lax.axis_index("gx")
        b = lax.axis_index("gy")
        up_a, dn_a = lax.rem(a + 1, n_gx), lax.rem(a + n_gx - 1, n_gx)
        up_b, dn_b = lax.rem(b + 1, n_gy), lax.rem(b + n_gy - 1, n_gy)

        barrier = pltpu.get_barrier_semaphore()
        for d in (up_a, dn_a):
            pl.semaphore_signal(barrier, inc=1, device_id=(d, b), device_id_type=MESH)

        def partner(i):
            half = lax.div(i + 1, 2)
            return n_gy // 2 + jnp.where(lax.rem(i, 2) == 1, half, -half)

        def greet(i, _):
            pl.semaphore_signal(
                barrier, inc=1, device_id=(a, lax.rem(b + partner(i), n_gy)), device_id_type=MESH
            )
            return 0

        lax.fori_loop(0, n_gy - 1, greet, 0)

        own = []
        for j in range(3):
            lanes = pl.ds(j * L, L)
            own.append(pltpu.make_async_copy(coarse.at[:, :, :, lanes], OWN.at[2:8, 0:SIDE, j, 0:F, :], in_sem.at[0, j]))
        for j in range(3):
            lanes = pl.ds(j * L, L)
            own.append(pltpu.make_async_copy(coarse.at[:, :, :, lanes], S.at[:, 2:8, j, 0:F, :], in_sem.at[1, j]))
        fin_cp = pltpu.make_async_copy(fine, FIN, fin_sem)
        tabs = [
            pltpu.make_async_copy(source.at[a], src_s, tab_sem.at[0]),
            pltpu.make_async_copy(live.at[a], live_s, tab_sem.at[1]),
        ]
        for cp in tabs + own[:1] + [fin_cp] + own[1:]:
            cp.start()

        for cp in tabs:
            cp.wait()

        def route(o, carry):
            owner, alive = carry
            d = lax.rem(b + o, n_gy)
            kf = jnp.int32(0)
            kg = jnp.int32(0)
            back = lax.rem(n_gy - o, n_gy)
            own_new, live_new = [], []
            for k in reversed(range(CAP)):
                kf = jnp.where((src_s[k, b] == d) & (live_s[k, b] == 1), k, kf)
                mine = src_s[k, d] == b
                lv = live_s[k, d]
                kg = jnp.where(mine & (lv == 1), k, kg)
                own_new.append(jnp.where(mine, back, owner[k]))
                live_new.append(jnp.where(mine, lv, alive[k]))
            kf_s[o] = kf
            kg_s[o] = kg
            return tuple(reversed(own_new)), tuple(reversed(live_new))

        zeros = (jnp.int32(0),) * CAP
        owner, alive = lax.fori_loop(0, n_gy, route, (zeros, zeros))

        lane = iota((8, L), 1)
        sub = iota((8, L), 0)
        lc = lane & 31
        ls = lane >> 5
        ly = jnp.where(
            lc < 4, lc + 1, jnp.where(lc < 8, lc - 3, jnp.where(lc < 12, 0, jnp.where(lc < 16, 5, ((lc - 16) >> 2) + 1)))
        )
        low16 = lc < 16

        lzc = jnp.where(
            lc < 4, 0, jnp.where(lc < 8, 5, jnp.where(lc < 12, lc - 7, jnp.where(lc < 16, lc - 11, (lc & 3) + 1)))
        )
        to_code = 6 * ls + lzc

        def merge(tile, X):
            acc = pick(tile(X + 1, 0), to_code)
            for y in range(1, 6):
                acc = jnp.where(low16 & (ly == y), pick(tile(X + 1, y), to_code), acc)
            if X in (0, 3):
                for y in range(1, 5):
                    part = pick(tile(0 if X == 0 else 5, y), to_code)
                    acc = jnp.where(jnp.logical_not(low16) & (ly == y), part, acc)
            return acc

        hole = (lane >= 48) & (lane < 64)
        from_lane = jnp.where(sub < 3, 16 * sub, jnp.where(sub == 3, 64, 16 * sub + 32))
        to_hole = jnp.where(hole & (sub < 6), from_lane + lane - 48, lane)
        from_hole = 48 + (lane & 15)
        part16 = lane >> 4
        from_row = jnp.where(
            part16 < 3, part16, jnp.where(part16 == 4, 3, jnp.where(part16 >= 6, part16 - 2, 8))
        )

        def pack(tile):
            return jnp.where(hole, pick(jnp.broadcast_to(tile[6:7], (8, L)), to_hole), tile)

        def unpack(tile):
            last = jnp.where(sub == from_row, pick(tile, from_hole), 0.0)
            for step in (4, 2, 1):
                last = last + pltpu.roll(last, step, 0)
            return jnp.where(sub == 6, last, tile)

        def ghost_messages(merged, dst, packed):
            for k in range(CAP):
                acc = None
                for X in range(4):
                    shift = (32 * (X - k)) % L
                    part = merged[X] if shift == 0 else pltpu.roll(merged[X], shift, 1)
                    acc = part if acc is None else jnp.where(ls == X, part, acc)
                dst[k] = acc
                packed[k] = pack(acc)

        own[0].wait()
        ghost_messages([merge(lambda x, y: OWN[x + 2, y, 0], X) for X in range(4)], MO, MOP)
        fin_cp.wait()
        for t in range(4 * CAP):
            FT[t // 4, t % 4, 0:F, :] = FIN[:, t * L : (t + 1) * L]

        RB0[0] = MOP[kg_s[0]]
        RB1[0] = FT[kf_s[0]]

        def fill(o, _):
            SB0[o] = MOP[kg_s[o]]
            SB1[o] = FT[kf_s[o]]
            return 0

        lax.fori_loop(1, n_gy, fill, 0)
        for cp in own[1:]:
            cp.wait()
        pl.semaphore_wait(barrier, n_gy + 1)

        def halo(lo, hi, sides=(0, 1, 2, 3)):
            copies = []
            for h, (buf, src, dst, dev) in enumerate(
                (
                    (OWN, OWN.at[6:8, 0:SIDE, lo:hi, 0:F, :], OWN.at[0:2, 0:SIDE, lo:hi, 0:F, :], (up_a, b)),
                    (OWN, OWN.at[2:4, 0:SIDE, lo:hi, 0:F, :], OWN.at[8:10, 0:SIDE, lo:hi, 0:F, :], (dn_a, b)),
                    (S, S.at[:, 6:8, lo:hi, 0:F, :], S.at[:, 0:2, lo:hi, 0:F, :], (a, up_b)),
                    (S, S.at[:, 2:4, lo:hi, 0:F, :], S.at[:, 8:10, lo:hi, 0:F, :], (a, dn_b)),
                )
            ):
                if h not in sides:
                    continue
                cp = pltpu.make_async_remote_copy(
                    src_ref=src,
                    dst_ref=dst,
                    send_sem=h_send.at[lo, h],
                    recv_sem=h_recv.at[lo, h],
                    device_id=dev,
                    device_id_type=MESH,
                )
                cp.start()
                copies.append(cp)
            return copies

        halos = halo(0, 1, (0, 1))

        def send_to_partners(src, dst, sem):
            def send(i, _):
                o = partner(i)
                pltpu.make_async_remote_copy(
                    src_ref=src(o),
                    dst_ref=dst(o),
                    send_sem=m_send.at[sem],
                    recv_sem=m_recv.at[sem],
                    device_id=(a, lax.rem(b + o, n_gy)),
                    device_id_type=MESH,
                ).start()
                return 0

            lax.fori_loop(0, n_gy - 1, send, 0)

        send_to_partners(lambda o: SB0.at[o, 0 : F - 1, :], lambda o: RB0.at[o, 0 : F - 1, :], 0)
        halos += halo(0, 1, (2, 3))
        send_to_partners(lambda o: SB1.at[o, :, 0:F, :], lambda o: RB1.at[o, :, 0:F, :], 1)
        halos_x = halo(1, 3, (0, 1))

        def cells(x, j):
            start = ((x + 2) * 24 + j) * 8
            return [take(OWN, start + f, 8, 24) for f in range(F)]

        def y_cells(x, y, j):
            start = ((x * 10 + y + 2) * 3 + j) * 8
            return [take(S, start + f, 8, 24) for f in range(F)]

        def x_split(x, j):
            return split_flux(cells(x - 1, j), cells(x, j), cells(x + 1, j), 0)

        def z_parts(j, _):
            jm, jp = lax.rem(j + 2, 3), lax.rem(j + 1, 3)
            for x in range(SIDE):
                mid = cells(x, j)
                um = [pltpu.roll(jnp.where(lane == L - 1, l, c), 1, 1) for l, c in zip(cells(x, jm), mid)]
                up = [pltpu.roll(jnp.where(lane == 0, r, c), L - 1, 1) for r, c in zip(cells(x, jp), mid)]
                plus, minus = split_flux(um, mid, up, 2)
                for f in range(F):
                    PZ[j, x, f] = plus[f]
                    MZ[j, x, f] = minus[f]
            return 0

        lax.fori_loop(0, 3, z_parts, 0)
        for x in range(1, 5):
            plus, minus = x_split(x, 0)
            for f in range(F):
                PX[x, f] = plus[f]
                MX[x, f] = minus[f]

        row = iota((L, L), 0)
        col = iota((L, L), 1)
        c32 = col & 31
        ry = (row >> 3) & 7
        rz = row & 7
        rzc, ryc = rz >> 1, ry >> 1
        e6 = (c32 * 43) >> 8
        eyv = jnp.where(c32 < 24, e6 + 1, jnp.where(c32 < 28, 0, 5))
        ezv = jnp.where(c32 < 24, c32 - 6 * e6, (c32 & 3) + 1)
        main = c32 < 24
        wa = main & (ezv >= 1) & (ezv <= 4) & (ryc == eyv - 1) & (rzc == ezv - 1)
        wz = main & (ryc == eyv - 1) & (((ezv == 0) & (rz == 0)) | ((ezv == 5) & (rz == 7)))
        wy = (
            jnp.logical_not(main)
            & (rzc == ezv - 1)
            & (((eyv == 0) & (ry == 0)) | ((eyv == 5) & (ry == 7)))
        )
        for i, w in enumerate((wa, wz, wy)):
            WD[i * L : (i + 1) * L, :] = jnp.where(w, 0.125, 0.0).astype(BF16)
        WX[...] = jnp.where((ryc == (c32 >> 2)) & (rzc == (c32 & 3)), 0.125, 0.0).astype(BF16)
        slot24 = (lane >= 6).astype(jnp.int32) + (lane >= 12).astype(jnp.int32) + (lane >= 18).astype(jnp.int32)
        zpos = lane - 6 * slot24
        alive_lane = jnp.where(
            slot24 == 0, alive[0], jnp.where(slot24 == 1, alive[1], jnp.where(slot24 == 2, alive[2], alive[3]))
        )
        live_z = (lane < 24) & (alive_lane == 1)
        zin = live_z & (zpos >= 1) & (zpos <= 4)
        yin = (sub >= 1) & (sub <= 4)
        inner = yin & zin
        y_low, y_high = (sub == 0) & zin, (sub == 5) & zin
        z_low, z_high = yin & live_z & (zpos == 0), yin & live_z & (zpos == 5)

        def y_parts(x, j):
            plus, minus = split_flux(y_cells(x, -2, j), y_cells(x, -1, j), y_cells(x, 0, j), 1)
            g = [p + pltpu.roll(m, 7, 0) for p, m in zip(plus, minus)]
            return g, [pltpu.roll(v, 7, 0) for v in g]

        def z_faces(x, f, j):
            jm, jp = lax.rem(j + 2, 3), lax.rem(j + 1, 3)
            p, m = PZ[j, x, f], MZ[j, x, f]
            upper = p + pltpu.roll(jnp.where(lane == 0, MZ[jp, x, f], m), L - 1, 1)
            lower = m + pltpu.roll(jnp.where(lane == L - 1, PZ[jm, x, f], p), 1, 1)
            return lower, upper

        def store(x, j, new):
            for f in range(F):
                put(BASE, (x * 24 + j) * 8 + f, 8, 24, new[f])

        zero = jnp.int32(0)
        halos[2].wait_recv()
        halos[3].wait_recv()
        for x in range(SIDE):
            y_lo, y_up = y_parts(x, 0)
            for f in range(F):
                z_lo, z_up = z_faces(x, f, zero)
                whole = (y_up[f] - y_lo[f]) + (z_up - z_lo)
                CH[x, f] = whole
                if 1 <= x <= 4:
                    whole = (jnp.where(y_low, 0.0, y_up[f]) - jnp.where(y_high, 0.0, y_lo[f])) + (
                        jnp.where(z_low, 0.0, z_up) - jnp.where(z_high, 0.0, z_lo)
                    )
                CM[x, f] = whole
        def face(plus, minus):
            return [p + m for p, m in zip(plus, minus)]

        def stored(buf, x):
            return [buf[x, f] for f in range(F)]

        def finish(x, lower, upper):
            new = react(cells(x, 0), [CH[x, f] + (upper[f] - lower[f]) for f in range(F)], 0.05)
            for f in range(F):
                put(NEWC, x * 64 + f, 8, 8, new[f])
                up_m, lo_m = upper[f], lower[f]
                if x == 0:
                    up_m = jnp.where(inner, 0.0, up_m)
                elif x == 5:
                    lo_m = jnp.where(inner, 0.0, lo_m)
                CM[x, f] = CM[x, f] + (up_m - lo_m)

        face12 = face(stored(PX, 1), stored(MX, 2))
        face23 = face(stored(PX, 2), stored(MX, 3))
        face34 = face(stored(PX, 3), stored(MX, 4))
        finish(2, face12, face23)
        finish(3, face23, face34)

        def new_tile(x, y):
            return NEWC[x, y]

        mid = [merge(new_tile, 1), merge(new_tile, 2)]
        halos[0].wait_recv()
        plus_m1, _ = x_split(-1, 0)
        plus_0, minus_0 = x_split(0, 0)
        face01 = face(plus_0, stored(MX, 1))
        finish(0, face(plus_m1, minus_0), face01)
        finish(1, face01, face(stored(PX, 1), stored(MX, 2)))
        first = merge(new_tile, 0)
        halos[1].wait_recv()
        plus_5, minus_5 = x_split(5, 0)
        _, minus_6 = x_split(6, 0)
        face45 = face(stored(PX, 4), minus_5)
        finish(4, face(stored(PX, 3), stored(MX, 4)), face45)
        finish(5, face45, face(plus_5, minus_6))
        ghost_messages([first] + mid + [merge(new_tile, 3)], MN, MNP)
        RB2[0] = MNP[kg_s[0]]
        for o in range(1, n_gy):
            SB2[o] = MNP[kg_s[o]]
        send_to_partners(lambda o: SB2.at[o, 0 : F - 1, :], lambda o: RB2.at[o, 0 : F - 1, :], 2)

        for x in range(SIDE):
            store(x, zero, react(cells(x, 0), [CM[x, f] for f in range(F)], 0.05))
        halos_y = halo(1, 3, (2, 3))
        for cp in halos_x:
            cp.wait_recv()

        def rest_xz(j, _):
            before = x_split(-1, j)[0]
            lower = None
            for x in range(SIDE + 1):
                plus, minus = x_split(x, j)
                upper = face(before, minus)
                if lower is not None:
                    for f in range(F):
                        z_lo, z_up = z_faces(x - 1, f, j)
                        CX[j, x - 1, f] = (upper[f] - lower[f]) + (z_up - z_lo)
                before, lower = plus, upper
            return 0

        lax.fori_loop(1, 3, rest_xz, 0)

        def wait_messages(whole, sem):
            pltpu.make_async_copy(whole, whole, sem).wait()

        my_src = [lax.rem(b + n_gy - src_s[k, b], n_gy) for k in range(CAP)]
        my_live = [live_s[k, b] for k in range(CAP)]

        tz, ty = lane & 7, (lane >> 3) & 7
        to_cell = (
            jnp.where(tz < 4, 0, 4) + (ty >> 1),
            jnp.where(ty < 4, 8, 12) + (tz >> 1),
            16 + (ty >> 1) * 4 + (tz >> 1),
        )

        def ghost_fields(messages):
            n = len(messages)
            for k in range(n):
                for X in range(4):
                    for i in range(3):
                        GG[i, (k * 4 + X) * 8 : (k * 4 + X) * 8 + 8] = pick(messages[k], to_cell[i] + 32 * X)
            return [[GG[i, pl.ds(f, 4 * n, stride=8), :] for f in range(F)] for i in range(3)]

        def lane_down(step):
            return lambda v: pltpu.roll(v, step, 1)

        def lane_up(step):
            return lambda v: pltpu.roll(v, L - step, 1)

        def substep(u, ghosts):
            R = u[0].shape[0]
            flane = iota((R, L), 1)
            frow = iota((R, L), 0) & 3
            z, y, odd = flane & 7, (flane >> 3) & 7, (flane >> 6) == 1
            even = jnp.logical_not(odd)

            def x_down(v):
                r = pltpu.roll(v, 64, 1)
                return jnp.where(odd, r, pltpu.roll(r, 1, 0))

            def x_up(v):
                r = pltpu.roll(v, 64, 1)
                return jnp.where(odd, pltpu.roll(r, R - 1, 0), r)

            plan = (
                (2, 0, lane_down(1), lane_up(1), z == 0, z == 7, z < 4),
                (1, 1, lane_down(8), lane_up(8), y == 0, y == 7, y < 4),
                (0, 2, x_down, x_up, (frow == 0) & even, (frow == 3) & odd, even),
            )
            change = None
            faces = []
            for d, gi, down, upw, at_lo, at_hi, lo_side in plan:
                g = ghosts[gi]
                um = [jnp.where(at_lo, w, down(c)) for c, w in zip(u, g)]
                up = [jnp.where(at_hi, w, upw(c)) for c, w in zip(u, g)]
                plus, minus = split_flux(um, u, up, d)
                sign = jnp.where(lo_side, 0.1, -0.1)
                edge = [h + sign * c for h, c in zip(half_flux(g, d), g)]
                lower, upper = [], []
                for f in range(F):
                    lower.append(minus[f] + jnp.where(at_lo, edge[f], down(plus[f])))
                    upper.append(plus[f] + jnp.where(at_hi, edge[f], upw(minus[f])))
                diff = [q - p for q, p in zip(upper, lower)]
                change = diff if change is None else [c + v for c, v in zip(change, diff)]
                faces.append(
                    [
                        jnp.where(at_lo[0:16], -p[0:16], jnp.where(at_hi[0:16], q[0:16], 0.0))
                        for q, p in zip(upper, lower)
                    ]
                )
            return react(u, change, 0.025), faces

        wait_messages(RB0.at[1:n_gy, 0 : F - 1, :], m_recv.at[0])
        for k in range(CAP):
            FS[CAP + k] = FT[k]
        u0 = [take(FS, CAP * 32 + f, 16, 8) for f in range(F)]
        u1, _ = substep(u0, ghost_fields([unpack(RB0[my_src[k]]) for k in range(CAP)]))
        for f in range(F):
            put(FS, CAP * 32 + f, 16, 8, u1[f])

        tile_old = ghost_fields([MO[k] for k in range(CAP)])
        wait_messages(RB1.at[1:n_gy, :, 0:F, :], m_recv.at[1])
        for k in range(CAP):
            FS[k] = RB1[owner[k]]
        u0 = [take(FS, f, 16, 8) for f in range(F)]
        u1, faces1 = substep(u0, tile_old)
        u2, faces2 = substep(u1, ghost_fields([0.5 * (MO[k] + MN[k]) for k in range(CAP)]))
        for f in range(F):
            rows = pl.ds(f, 16, stride=8)
            LW[0, rows, :] = u2[f]
            for i in range(3):
                LW[1 + i, rows, :] = faces1[i][f] + faces2[i][f]

        TT[0] = exact_dot(jnp.concatenate([LW[0], LW[1], LW[2]], axis=1), WD[...])
        TT[1] = exact_dot(LW[3], WX[...])
        slot_live = jnp.where(ls == 0, alive[0], jnp.where(ls == 1, alive[1], jnp.where(ls == 2, alive[2], alive[3])))
        keep = slot_live == 1

        def by_slot(i, X):
            acc = TT[i, pl.ds(X * 8, 8), :]
            for k in range(1, CAP):
                acc = jnp.where(ls == k, TT[i, pl.ds((k * 4 + X) * 8, 8), :], acc)
            return jnp.where(keep, acc, 0.0)

        z_mid = (lane < 24) & (zpos >= 1) & (zpos <= 4)
        base_code = jnp.where(lane < 24, 32 * slot24, 0)
        tt = [by_slot(0, X) for X in range(4)]
        tx = {0: by_slot(1, 0), 5: by_slot(1, 3)}
        for x in range(SIDE):
            for y in range(SIDE):
                tile = BASE[x, y, 0]
                if 1 <= x <= 4:
                    if 1 <= y <= 4:
                        part = pick(tt[x - 1], base_code + jnp.where(lane < 24, (y - 1) * 6 + zpos, 0))
                        tile = jnp.where(zin, part, jnp.where(lane < 24, tile + part, tile))
                    else:
                        code = (24 if y == 0 else 28) + jnp.where(z_mid, zpos - 1, 0)
                        tile = jnp.where(z_mid, tile + pick(tt[x - 1], base_code + code), tile)
                elif 1 <= y <= 4:
                    code = (y - 1) * 4 + jnp.where(z_mid, zpos - 1, 0)
                    tile = jnp.where(z_mid, tile + pick(tx[x], base_code + code), tile)
                coarse_out[x, y, :, 0:L] = tile[0:F]

        for cp in halos_y:
            cp.wait_recv()

        def rest_y(j, _):
            for x in range(SIDE):
                y_lo, y_up = y_parts(x, j)
                change = [CX[j, x, f] + (y_up[f] - y_lo[f]) for f in range(F)]
                store(x, j, react(cells(x, j), change, 0.05))
            return 0

        lax.fori_loop(1, 3, rest_y, 0)
        for x in range(SIDE):
            for y in range(SIDE):
                for j in (1, 2):
                    coarse_out[x, y, :, j * L : (j + 1) * L] = BASE[x, y, j, 0:F]

        wait_messages(RB2.at[1:n_gy, 0 : F - 1, :], m_recv.at[2])
        mean = [unpack(0.5 * (RB0[my_src[k]] + RB2[my_src[k]])) for k in range(CAP)]
        u1 = [take(FS, CAP * 32 + f, 16, 8) for f in range(F)]
        u2, _ = substep(u1, ghost_fields(mean))
        for f in range(F):
            put(FS, CAP * 32 + f, 16, 8, u2[f])
        for t in range(4 * CAP):
            k = t // 4
            fine_out[:, t * L : (t + 1) * L] = jnp.where(
                my_live[k] == 1, FS[CAP + k, t % 4, 0:F, :], FT[k, t % 4, 0:F, :]
            )

        for cp in halos + halos_x + halos_y:
            cp.wait_send()
        wait_messages(SB0.at[1:n_gy, 0 : F - 1, :], m_send.at[0])
        wait_messages(SB1.at[1:n_gy, :, 0:F, :], m_send.at[1])
        wait_messages(SB2.at[1:n_gy, 0 : F - 1, :], m_send.at[2])

    return kernel


def hand_over(coarse, fine, coarse_out, fine_out, sem):
    copies = [
        pltpu.make_async_copy(coarse, coarse_out, sem.at[0]),
        pltpu.make_async_copy(fine, fine_out, sem.at[1]),
    ]
    for cp in copies:
        cp.start()
    for cp in copies:
        cp.wait()


def solution(mesh):
    n_gx, n_gy = mesh.shape["gx"], mesh.shape["gy"]
    kernel = make_kernel(n_gx, n_gy)

    def local(coarse_state, fine_state, patch_source, patch_live):
        coarse = jnp.transpose(coarse_state, (1, 2, 0, 3))
        source = jnp.transpose(patch_source, (0, 2, 1))
        live = jnp.transpose(patch_live, (0, 2, 1))
        coarse, fine, source, live = (
            pltpu.with_memory_space_constraint(v, pltpu.HBM) for v in (coarse, fine_state, source, live)
        )
        v = pltpu.VMEM
        hbm = pl.BlockSpec(memory_space=pltpu.HBM)
        vmem = pl.BlockSpec(memory_space=pltpu.VMEM)
        coarse_out, fine_out = pl.pallas_call(
            kernel,
            out_shape=(
                pltpu.VMEM(coarse.shape, F32),
                pltpu.VMEM(fine_state.shape, F32),
            ),
            in_specs=[hbm] * 4,
            out_specs=(vmem, vmem),
            scratch_shapes=[
                v((SIDE, 10, 3, 8, L), F32),
                v((10, 8, 3, 8, L), F32),
                v((F, 4 * CAP * L), F32),
                v((SIDE, 8, 3, 8, L), F32),
                v((SIDE, 8, 8, L), F32),
                v((3, SIDE, F, 8, L), F32),
                v((3, SIDE, F, 8, L), F32),
                v((SIDE, F, 8, L), F32),
                v((SIDE, F, 8, L), F32),
                v((SIDE, F, 8, L), F32),
                v((SIDE, F, 8, L), F32),
                v((3, SIDE, F, 8, L), F32),
                v((CAP, 8, L), F32),
                v((CAP, 8, L), F32),
                v((CAP, 8, L), F32),
                v((CAP, 8, L), F32),
                v((2 * CAP, 4, 8, L), F32),
                v((CAP, 4, 8, L), F32),
                v((3, 2 * CAP * 32, L), F32),
                v((n_gy, 8, L), F32),
                v((n_gy, 8, L), F32),
                v((n_gy, 4, 8, L), F32),
                v((n_gy, 4, 8, L), F32),
                v((n_gy, 8, L), F32),
                v((n_gy, 8, L), F32),
                v((3 * L, L), BF16),
                v((L, L), BF16),
                v((4, CAP * 32, L), F32),
                v((2, CAP * 32, L), F32),
                pltpu.SMEM((CAP, n_gy), jnp.int32),
                pltpu.SMEM((CAP, n_gy), jnp.int32),
                pltpu.SMEM((n_gy,), jnp.int32),
                pltpu.SMEM((n_gy,), jnp.int32),
                pltpu.SemaphoreType.DMA((2, 3)),
                pltpu.SemaphoreType.DMA,
                pltpu.SemaphoreType.DMA((2,)),
                pltpu.SemaphoreType.DMA((2, 4)),
                pltpu.SemaphoreType.DMA((2, 4)),
                pltpu.SemaphoreType.DMA((3,)),
                pltpu.SemaphoreType.DMA((3,)),
            ],
            compiler_params=pltpu.CompilerParams(
                collective_id=0, has_side_effects=True, vmem_limit_bytes=48 * 2**20
            ),
        )(coarse, fine, source, live)
        coarse_out, fine_out = (
            pltpu.with_memory_space_constraint(v, pltpu.VMEM) for v in (coarse_out, fine_out)
        )
        coarse_out, fine_out = pl.pallas_call(
            hand_over,
            out_shape=(
                jax.ShapeDtypeStruct(coarse.shape, F32),
                jax.ShapeDtypeStruct(fine_state.shape, F32),
            ),
            in_specs=[vmem] * 2,
            out_specs=(hbm, hbm),
            scratch_shapes=[pltpu.SemaphoreType.DMA((2,))],
        )(coarse_out, fine_out)
        return jnp.transpose(coarse_out, (2, 0, 1, 3)), fine_out

    return jax.shard_map(
        local,
        mesh=mesh,
        in_specs=(P(None, "gx", "gy", None), P(None, ("gx", "gy")), P(), P()),
        out_specs=(P(None, "gx", "gy", None), P(None, ("gx", "gy"))),
        check_vma=False,
    )
```
